256 devices in a mesh: leaf: 256 (over z, x, y, core).
Axes of the slice: x: 4, y: 4, z: 8, core: 2. Of those that a mesh axis runs over, the one named last changes fastest.
Arguments:
- charges: bfloat16 [16, 2097152], P(None, 'leaf'), may hold values from -6 to 6
- points: bfloat16 [3, 2097152], P(None, 'leaf'), may hold values from 0 to 1
- leaf_basis: bfloat16 [2048, 1024, 128], P('leaf'), may hold values from -0.1875 to 0.1875
- transfer: float32 [4, 2, 128, 128], replicated, may hold values from -0.375 to 0.375
- coupling: float32 [4, 3, 128, 128], replicated, may hold values from -0.5 to 0.5
- near_list: int32 [2048, 5], P('leaf'), may hold values from 0 to 2047, as said below
- couple_flags: int32 [256, 4, 3], P('leaf'), may hold values from 0 to 1, as said below
Outputs:
- potential: bfloat16 [16, 2097152], P(None, 'leaf')
The draws below stay inside these ranges and needn't reach their ends.
Inputs may be any that keep to these rules, and one draw needn't show every extreme that they name: `near_list`: entries of a row are distinct leaves within 32 of the row's leaf i; the first is i itself and the second lies exactly 32 away from i. `couple_flags`: at level t the flags are equal for all clusters c with equal c // 2^t.
All inputs are finite; a program needn't handle non-finite values.
Results may differ from the reference program's by a relative error of at most 0.0049.
Values may be sent and summed in bfloat16 or wider, within the bound.
No kernel may reach another device: no remote copies, remote signals or barrier semaphores. Data moves between devices by JAX's collectives and lax.ppermute only.
A program may use at most 64 MiB of HBM per device.

```python
import math
import jax
import jax.numpy as jnp
from jax import lax

LEAF = 1024
RANK = 128
RHS = 16
NB = 5
LEVELS = 4
LEAVES_DEV = 8
RADIUS = 32
CLUSTERS = 256
LEAVES = 2048
ROWS = 2097152


def draw_near_list(key, part):
    key = jax.random.fold_in(key, 11)
    span = 2 * RADIUS + 1
    offsets = jnp.arange(-RADIUS, RADIUS + 1, dtype=jnp.int32)
    leaf_ids = jnp.arange(LEAVES, dtype=jnp.int32)[:, None]
    candidates = leaf_ids + offsets[None, :]
    inside = (candidates >= 0) & (candidates < LEAVES)
    far_leaf = jnp.where(leaf_ids[:, 0] + RADIUS < LEAVES, leaf_ids[:, 0] + RADIUS, leaf_ids[:, 0] - RADIUS)
    scores = jax.random.randint(key, (LEAVES, span), 0, 2 ** 20) * span + jnp.arange(span, dtype=jnp.int32)[None, :]
    usable = inside & (candidates != leaf_ids) & (candidates != far_leaf[:, None])
    scores = jnp.where(usable, scores, -1)
    unused, chosen_cols = lax.top_k(scores, NB - 2)
    chosen = jnp.take_along_axis(candidates, chosen_cols, axis=1)
    return jnp.concatenate([leaf_ids, far_leaf[:, None], chosen], axis=1).astype(jnp.int32)


def draw_couple_flags(key, part):
    key = jax.random.fold_in(key, 12)
    random_bits = jax.random.randint(key, (CLUSTERS, LEVELS, 3), 0, 2)
    node_ids = jnp.arange(CLUSTERS, dtype=jnp.int32)
    per_level = [random_bits[node_ids // 2 ** t * 2 ** t, t] for t in range(LEVELS)]
    return jnp.stack(per_level, axis=1).astype(jnp.int32)


def level_of(rng, extent, shards, least, largest):
    def one(axis_at, blocks):
        draws = jax.random.uniform(jax.random.fold_in(jax.random.fold_in(rng, 6), axis_at), (blocks,), jnp.float32, least / len(shards), largest / len(shards))
        return jnp.repeat(jnp.exp(draws), extent[axis_at] // blocks).reshape((-1,) + (1,) * (len(extent) - axis_at - 1))

    loudness = one(*shards[0])
    for cut in shards[1:]:
        loudness = loudness * one(*cut)
    return loudness


def normal_values(stream_key, extent, deviation, bound, cuts=(), kind=jnp.bfloat16):
    entries = jax.random.normal(stream_key, extent, jnp.float32) * deviation
    if len(cuts) > 0:
        entries = level_of(stream_key, extent, cuts, -0.22, 0.18) * entries
    return jnp.clip(entries, min=-bound, max=bound).astype(kind)


def setup_inputs(seed: int = 0) -> dict:
    key_list = jax.random.split(jax.random.key(seed), 8)
    charges = normal_values(key_list[0], (RHS, ROWS), 1.0, 6.0, ((1, 256),))
    points = jnp.clip(1.0 * jax.random.uniform(key_list[1], (3, ROWS), jnp.float32) ** level_of(key_list[1], (3, ROWS), ((1, 256),), -0.2, 0.2), 0.0, 1.0).astype(jnp.bfloat16)
    leaf_basis = normal_values(key_list[2], (LEAVES, LEAF, RANK), LEAF ** -0.5, 0.1875, ((0, 256),))
    transfer = normal_values(key_list[3], (LEVELS, 2, RANK, RANK), (2 * RANK) ** -0.5, 0.375, (), jnp.float32)
    coupling = normal_values(key_list[4], (LEVELS, 3, RANK, RANK), RANK ** -0.5, 0.5, (), jnp.float32)
    near_list = draw_near_list(jax.random.fold_in(key_list[7], 71), 0)
    couple_flags = draw_couple_flags(jax.random.fold_in(key_list[7], 71), 0)
    return dict(charges=charges, points=points, leaf_basis=leaf_basis, transfer=transfer, coupling=coupling, near_list=near_list, couple_flags=couple_flags)


smoothing_sq = 0.01

def positions(raw, leaf_num, leaf_step):
    coords = raw.astype(jnp.float32)
    return jnp.stack([coords[0] + leaf_num * leaf_step, coords[1], coords[2]], axis=0)

def kernel_block(src_pos, tgt_pos):
    diff_x = src_pos[0][:, None] - tgt_pos[0][None, :]
    diff_y = src_pos[1][:, None] - tgt_pos[1][None, :]
    diff_z = src_pos[2][:, None] - tgt_pos[2][None, :]
    dist_sq = diff_x * diff_x + diff_y * diff_y + diff_z * diff_z
    return lax.rsqrt(dist_sq + smoothing_sq).astype(jnp.bfloat16)

def reference(charges, points, leaf_basis, transfer, coupling, near_list, couple_flags):
    highest = lax.Precision.HIGHEST
    cluster_rows = LEAVES_DEV * LEAF
    leaf_step = 1.0 / (2.0 * RADIUS)

    def near_leaf(i):
        tgt_pos = positions(lax.dynamic_slice(points, (jnp.int32(0), i * LEAF), (3, LEAF)), i.astype(jnp.float32), leaf_step)
        near_sum = jnp.zeros((RHS, LEAF), jnp.float32)
        for k in range(NB):
            j = near_list[i, k].astype(jnp.int32)
            src_pos = positions(lax.dynamic_slice(points, (jnp.int32(0), j * LEAF), (3, LEAF)), j.astype(jnp.float32), leaf_step)
            src_vals = lax.dynamic_slice(charges, (jnp.int32(0), j * LEAF), (RHS, LEAF))
            near_sum = near_sum + jnp.dot(src_vals, kernel_block(src_pos, tgt_pos), preferred_element_type=jnp.float32)
        return near_sum
    near_field = lax.map(near_leaf, jnp.arange(LEAVES, dtype=jnp.int32))
    near_field = jnp.transpose(near_field, (1, 0, 2)).reshape(RHS, ROWS)

    def cluster_basis(c):
        return lax.dynamic_slice_in_dim(leaf_basis, c * LEAVES_DEV, LEAVES_DEV, 0).reshape(cluster_rows, RANK)

    def upward_leaf(c):
        src_vals = lax.dynamic_slice(charges, (jnp.int32(0), c * cluster_rows), (RHS, cluster_rows))
        return jnp.dot(src_vals, cluster_basis(c), preferred_element_type=jnp.float32)
    level_coef = lax.map(upward_leaf, jnp.arange(CLUSTERS, dtype=jnp.int32))
    coupled_levels = []
    for t in range(LEVELS):
        count = level_coef.shape[0]
        node_ids = jnp.arange(count, dtype=jnp.int32)
        coupled = jnp.zeros((count, RHS, RANK), jnp.float32)
        for m in range(1, 4):
            partner = level_coef[jnp.bitwise_xor(node_ids, m)]
            flag_vals = couple_flags[node_ids * 2 ** t, t, m - 1].astype(jnp.float32)
            product = jnp.einsum('nrk,kl->nrl', partner, coupling[t, m - 1], precision=highest)
            coupled = coupled + flag_vals[:, None, None] * product
        coupled_levels.append(coupled)
        if t + 1 < LEVELS:
            level_coef = jnp.einsum('nrk,kl->nrl', level_coef[0::2], transfer[t, 0], precision=highest) + jnp.einsum('nrk,kl->nrl', level_coef[1::2], transfer[t, 1], precision=highest)
    local_coef = coupled_levels[-1]
    for t in range(LEVELS - 1, 0, -1):
        down_left = jnp.einsum('nrl,kl->nrk', local_coef, transfer[t - 1, 0], precision=highest)
        down_right = jnp.einsum('nrl,kl->nrk', local_coef, transfer[t - 1, 1], precision=highest)
        count = local_coef.shape[0]
        spread = jnp.stack([down_left, down_right], axis=1).reshape(2 * count, RHS, RANK)
        local_coef = coupled_levels[t - 1] + spread
    local_bf = local_coef.astype(jnp.bfloat16)

    def far_leaf(c):
        return lax.dot_general(local_bf[c], cluster_basis(c), (((1,), (1,)), ((), ())), preferred_element_type=jnp.float32)
    far_field = lax.map(far_leaf, jnp.arange(CLUSTERS, dtype=jnp.int32))
    far_field = jnp.transpose(far_field, (1, 0, 2)).reshape(RHS, ROWS)
    near_scale = 1.0 / math.sqrt(NB * LEAF)
    return (near_field * near_scale + far_field).astype(jnp.bfloat16)
```

```python
import functools
import math

import jax
import jax.numpy as jnp
from jax import lax
from jax.experimental import pallas as pl
from jax.experimental.pallas import tpu as pltpu
from jax.sharding import PartitionSpec as P

bf16 = jnp.bfloat16
f32 = jnp.float32
smoothing_sq = 0.01
LEAF = 1024
HALF = 512
LEAVES_DEV = 8
RHS = 16
RANK = 128
NB = 5
FEATS = 16
PAYLOAD = (19, 16, HALF)
VM = pl.BlockSpec(memory_space=pltpu.VMEM)
SM = pl.BlockSpec(memory_space=pltpu.SMEM)
ANY = pl.BlockSpec(memory_space=pl.ANY)


def params(mib):
    return pltpu.CompilerParams(vmem_limit_bytes=mib * 2**20)


def permuted(array, source_of):
    count = lax.axis_size("leaf")
    route = [(source_of(i), i) for i in range(count) if 0 <= source_of(i) < count]
    return lax.ppermute(array, "leaf", route)


def pack_kernel(charges, points, out, rows):
    for k in range(16):
        out[k] = charges[:, k * HALF : (k + 1) * HALF]
    for l in range(LEAVES_DEV):
        for h in range(2):
            start = l * LEAF + h * HALF
            part = points[:, start : start + HALF].astype(f32)
            for c in range(3):
                row = h * 24 + c * 8 + l
                rows[row : row + 1, :] = part[c : c + 1]
    for k in range(3):
        out[16 + k] = rows[k * 16 : (k + 1) * 16, :].astype(bf16)


def pack(charges, points):
    return pl.pallas_call(
        pack_kernel,
        out_shape=jax.ShapeDtypeStruct(PAYLOAD, bf16),
        in_specs=[VM, VM],
        out_specs=VM,
        scratch_shapes=[pltpu.VMEM((48, HALF), f32)],
        compiler_params=params(16),
        cost_estimate=pl.CostEstimate(flops=10**6, bytes_accessed=10**6, transcendentals=0),
    )(charges, points)


def coordinates(block):
    rows = jnp.concatenate([block[16], block[17], block[18]], axis=0).astype(f32)
    return jnp.concatenate([rows[:24], rows[24:]], axis=1)


def squared_norm_parts(block, first_leaf, extra):
    pts = coordinates(block)
    leaf = lax.broadcasted_iota(jnp.int32, (LEAVES_DEV, LEAF), 0) + first_leaf
    a = leaf.astype(f32) * (1.0 / 64.0)
    x, y, z = pts[0:8], pts[8:16], pts[16:24]
    full_x = x + a
    norm = full_x * full_x + y * y + z * z + extra
    high = norm.astype(bf16).astype(f32)
    rest = norm - high
    middle = rest.astype(bf16).astype(f32)
    return x, a, y, z, high, middle, rest - middle


def store_features(dst, base, rows, tmp):
    for f, row in enumerate(rows):
        tmp[:, f, :] = row
    for f in range(len(rows), FEATS):
        tmp[:, f, :] = jnp.zeros((LEAVES_DEV, LEAF), f32)
    for l in range(LEAVES_DEV):
        dst[base + l] = tmp[l].astype(bf16)


def source_features(block, first_leaf, dst, base, tmp):
    x, a, y, z, high, middle, low = squared_norm_parts(block, first_leaf, 0.0)
    one = jnp.ones_like(x)
    store_features(dst, base, [x, x, a, a, y, z, high, middle, low, one, one, one], tmp)


def target_features(block, dst, tmp):
    x, a, y, z, high, middle, low = squared_norm_parts(block, 0, smoothing_sq)
    one = jnp.ones_like(x)
    rows = [-2 * x, -2 * a, -2 * x, -2 * a, -2 * y, -2 * z, one, one, one, high, middle, low]
    store_features(dst, 0, rows, tmp)


def near_kernel(stage, shapes, *refs):
    (place, near_list), refs = refs[:2], refs[2:]
    pieces, refs = refs[: len(shapes)], refs[len(shapes) :]
    if stage == 0:
        (acc, tgt, vals, feats, tmp) = refs
    elif stage == 1:
        (tgt, acc_in, acc, vals, feats, tmp) = refs
    else:
        (tgt, acc_in, down, basis_hbm, out, vals, feats, tmp, acc, basis, sem) = refs
        fetch = pltpu.make_async_copy(basis_hbm, basis, sem)
        fetch.start()
    me, sign = place[0], place[1]
    offsets = ((0, 1), (-1, -2, 2, 3), (-3, -4, 4))[stage]
    slot = 0
    for piece, shape in zip(pieces, shapes):
        for part in range(shape[0]):
            block = piece.at[part]
            for l in range(LEAVES_DEV):
                vals[slot * 8 + l, :, :HALF] = block[2 * l]
                vals[slot * 8 + l, :, HALF:] = block[2 * l + 1]
            source_features(
                block, offsets[slot] * sign * LEAVES_DEV, feats, slot * LEAVES_DEV, tmp
            )
            slot += 1
    if stage == 0:
        target_features(pieces[0].at[0], tgt, tmp)
        acc[...] = jnp.zeros_like(acc)
    else:
        acc[...] = acc_in[...]

    def add_block(i, w):
        src = feats[w].astype(f32).T.astype(bf16)
        for t in range(0, LEAF, 512):
            dist_sq = jnp.dot(src, tgt[i, :, t : t + 512], preferred_element_type=f32)
            kernel_vals = lax.rsqrt(dist_sq).astype(bf16)
            acc[i, :, t : t + 512] += jnp.dot(
                vals[w], kernel_vals, preferred_element_type=f32
            )

    first = {0: 0, 1: 1, 2: 1}[stage]

    def item(it, carry):
        i, k = it // NB, it % NB
        j = near_list[i, k]
        off = (j // LEAVES_DEV - me) * sign
        index = jnp.int32(-1)
        for s, o in enumerate(offsets):
            index = jnp.where(off == o, s, index)

        @pl.when(index >= 0)
        def _():
            add_block(i, index * LEAVES_DEV + j % LEAVES_DEV)

        return carry

    lax.fori_loop(0, LEAVES_DEV * NB, item, 0)
    if stage == 2:
        fetch.wait()
        scale = 1.0 / math.sqrt(NB * LEAF)
        for l in range(LEAVES_DEV):
            far = lax.dot_general(
                down[...], basis[l], (((1,), (1,)), ((), ())), preferred_element_type=f32
            )
            out[:, l * LEAF : (l + 1) * LEAF] = (acc[l] * scale + far).astype(bf16)


def near_stage(stage, place, near_list, pieces, *more):
    shapes = [p.shape for p in pieces]
    slots = sum(s[0] for s in shapes)
    acc = jax.ShapeDtypeStruct((LEAVES_DEV, RHS, LEAF), f32)
    tgt = jax.ShapeDtypeStruct((LEAVES_DEV, FEATS, LEAF), bf16)
    scratch = [
        pltpu.VMEM((slots * 8, RHS, LEAF), bf16),
        pltpu.VMEM((slots * 8, FEATS, LEAF), bf16),
        pltpu.VMEM((LEAVES_DEV, FEATS, LEAF), f32),
    ]
    specs = [SM, SM] + [VM] * len(pieces)
    if stage == 0:
        out_shape, out_specs = (acc, tgt), (VM, VM)
    elif stage == 1:
        out_shape, out_specs = acc, VM
        specs += [VM, VM]
    else:
        out_shape, out_specs = jax.ShapeDtypeStruct((RHS, LEAVES_DEV * LEAF), bf16), VM
        specs += [VM, VM, VM, ANY]
        scratch += [
            pltpu.VMEM((LEAVES_DEV, RHS, LEAF), f32),
            pltpu.VMEM((LEAVES_DEV, LEAF, RANK), bf16),
            pltpu.SemaphoreType.DMA,
        ]
    return pl.pallas_call(
        functools.partial(near_kernel, stage, shapes),
        out_shape=out_shape,
        in_specs=specs,
        out_specs=out_specs,
        scratch_shapes=scratch,
        compiler_params=params(40),
        cost_estimate=pl.CostEstimate(
            flops=10**10, bytes_accessed=10**6, transcendentals=13 * 10**6
        ),
    )(place, near_list, *pieces, *more)


def tree_kernel(place, flags, coefs, transfer, coupling, out):
    me = place[0]

    def dot(a, b):
        return jnp.dot(a, b, precision=lax.Precision.HIGHEST, preferred_element_type=f32)

    levels = 4
    cur = [coefs[m] for m in range(32)]
    coupled = []
    for t in range(levels):
        total = jnp.zeros((RHS, RANK), f32)
        for m in range(3):
            flag = flags[t, m].astype(f32)
            total = total + flag * dot(cur[m + 1], coupling[t, m])
        coupled.append(total)
        if t + 1 < levels:
            right = ((me >> t) & 1) == 1
            even = jnp.concatenate(cur[0::2], axis=0)
            odd = jnp.concatenate(cur[1::2], axis=0)
            merged = dot(jnp.where(right, odd, even), transfer[t, 0]) + dot(
                jnp.where(right, even, odd), transfer[t, 1]
            )
            cur = [merged[m * RHS : (m + 1) * RHS] for m in range(len(cur) // 2)]
    local = coupled[-1]
    for t in range(levels - 1, 0, -1):
        right = ((me >> (t - 1)) & 1) == 1
        mat = jnp.where(right, transfer[t - 1, 1], transfer[t - 1, 0])
        local = coupled[t - 1] + lax.dot_general(
            local,
            mat,
            (((1,), (1,)), ((), ())),
            precision=lax.Precision.HIGHEST,
            preferred_element_type=f32,
        )
    out[...] = local.astype(bf16)


def tree(place, flags, coefs, transfer, coupling):
    return pl.pallas_call(
        tree_kernel,
        out_shape=jax.ShapeDtypeStruct((RHS, RANK), bf16),
        in_specs=[SM, SM, VM, VM, VM],
        out_specs=VM,
        compiler_params=params(16),
        cost_estimate=pl.CostEstimate(flops=10**9, bytes_accessed=10**6, transcendentals=0),
    )(place, flags, coefs, transfer, coupling)


def local(charges, points, leaf_basis, transfer, coupling, near_list, couple_flags):
    me = lax.axis_index("leaf")
    sign = 1 - 2 * (me % 2)
    place = jnp.stack([me, sign]).astype(jnp.int32)

    own = pack(charges, points)
    sib = permuted(own, lambda i: i ^ 1)
    pair = jnp.stack([own, sib])
    near1 = permuted(pair, lambda i: i - 1 if i % 2 == 0 else i + 1)
    far1 = permuted(near1, lambda i: i - 2 if i % 2 == 0 else i + 2)
    near2 = permuted(near1, lambda i: i ^ 1)
    far2 = permuted(far1[:1], lambda i: i ^ 1)

    coefs = jnp.dot(
        charges,
        leaf_basis.reshape(LEAVES_DEV * LEAF, RANK),
        preferred_element_type=f32,
    )[None]
    for step in range(5):
        coefs = jnp.concatenate([coefs, permuted(coefs, lambda i: i ^ (1 << step))])

    acc, tgt = near_stage(0, place, near_list, [pair])
    acc = near_stage(1, place, near_list, [near1, near2], tgt, acc)
    down = tree(place, couple_flags[0], coefs, transfer, coupling)
    return near_stage(2, place, near_list, [far1, far2], tgt, acc, down, leaf_basis)


def solution(mesh):
    return jax.shard_map(
        local,
        mesh=mesh,
        in_specs=(
            P(None, "leaf"),
            P(None, "leaf"),
            P("leaf", None, None),
            P(),
            P(),
            P("leaf", None),
            P("leaf", None, None),
        ),
        out_specs=P(None, "leaf"),
        check_vma=False,
    )
```

```python
import functools
import math

import jax
import jax.numpy as jnp
from jax import lax
from jax.experimental import pallas as pl
from jax.experimental.pallas import tpu as pltpu
from jax.sharding import PartitionSpec as P

bf16 = jnp.bfloat16
f32 = jnp.float32
smoothing_sq = 0.01
LEAF = 1024
HALF = 512
LEAVES_DEV = 8
RHS = 16
RANK = 128
NB = 5
FEATS = 16
PAYLOAD = (19, 16, HALF)
VM = pl.BlockSpec(memory_space=pltpu.VMEM)
SM = pl.BlockSpec(memory_space=pltpu.SMEM)
SLOT_OFFSETS = (0, 1, -1, -2, 2, 3, -3, -4, 4)
SELF = (2, 4, 6, 8)
BUDGET = 11


def params(mib):
    return pltpu.CompilerParams(vmem_limit_bytes=mib * 2**20)


def permuted(array, source_of):
    count = lax.axis_size("leaf")
    route = [(source_of(i), i) for i in range(count) if 0 <= source_of(i) < count]
    return lax.ppermute(array, "leaf", route)


def pack_kernel(charges, points, out, rows):
    for k in range(16):
        out[k] = charges[:, k * HALF : (k + 1) * HALF]
    for l in range(LEAVES_DEV):
        for h in range(2):
            start = l * LEAF + h * HALF
            part = points[:, start : start + HALF].astype(f32)
            for c in range(3):
                row = h * 24 + c * 8 + l
                rows[row : row + 1, :] = part[c : c + 1]
    for k in range(3):
        out[16 + k] = rows[k * 16 : (k + 1) * 16, :].astype(bf16)


def pack(charges, points):
    return pl.pallas_call(
        pack_kernel,
        out_shape=jax.ShapeDtypeStruct(PAYLOAD, bf16),
        in_specs=[VM, VM],
        out_specs=VM,
        scratch_shapes=[pltpu.VMEM((48, HALF), f32)],
        compiler_params=params(16),
        cost_estimate=pl.CostEstimate(flops=10**6, bytes_accessed=10**6, transcendentals=0),
    )(charges, points)


def coordinates(block):
    rows = jnp.concatenate([block[16], block[17], block[18]], axis=0).astype(f32)
    return jnp.concatenate([rows[:24], rows[24:]], axis=1)


def squared_norm_parts(block, first_leaf, extra):
    pts = coordinates(block)
    leaf = lax.broadcasted_iota(jnp.int32, (LEAVES_DEV, LEAF), 0) + first_leaf
    a = leaf.astype(f32) * (1.0 / 64.0)
    x, y, z = pts[0:8], pts[8:16], pts[16:24]
    full_x = x + a
    norm = full_x * full_x + y * y + z * z + extra
    high = norm.astype(bf16).astype(f32)
    rest = norm - high
    middle = rest.astype(bf16).astype(f32)
    return x, a, y, z, high, middle, rest - middle


def store_features(dst, base, rows, tmp):
    for f, row in enumerate(rows):
        tmp[:, f, :] = row
    for f in range(len(rows), FEATS):
        tmp[:, f, :] = jnp.zeros((LEAVES_DEV, LEAF), f32)
    for l in range(LEAVES_DEV):
        dst[base + l] = tmp[l].astype(bf16)


def source_features(block, first_leaf, dst, base, tmp):
    x, a, y, z, high, middle, low = squared_norm_parts(block, first_leaf, 0.0)
    one = jnp.ones_like(x)
    store_features(dst, base, [x, x, a, a, y, z, high, middle, low, one, one, one], tmp)


def target_features(block, dst, tmp):
    x, a, y, z, high, middle, low = squared_norm_parts(block, 0, smoothing_sq)
    one = jnp.ones_like(x)
    rows = [-2 * x, -2 * a, -2 * x, -2 * a, -2 * y, -2 * z, one, one, one, high, middle, low]
    store_features(dst, 0, rows, tmp)


def load_cluster(block, slot, sign, vals, feats, tmp):
    for l in range(LEAVES_DEV):
        vals[slot * LEAVES_DEV + l, :, :HALF] = block[2 * l]
        vals[slot * LEAVES_DEV + l, :, HALF:] = block[2 * l + 1]
    first_leaf = SLOT_OFFSETS[slot] * LEAVES_DEV * sign
    source_features(block, first_leaf, feats, slot * LEAVES_DEV, tmp)


def add_block(i, w, tgt, vals, feats, acc):
    src = feats[w].astype(f32).T.astype(bf16)
    for t in range(0, LEAF, 512):
        dist_sq = jnp.dot(src, tgt[i, :, t : t + 512], preferred_element_type=f32)
        kernel_vals = lax.rsqrt(dist_sq).astype(bf16)
        acc[i, :, t : t + 512] += jnp.dot(vals[w], kernel_vals, preferred_element_type=f32)


def add_listed(part, work, tgt, vals, feats, acc):
    def item(it, count):
        i, k = it // (NB - 1), it % (NB - 1) + 1
        w = work[i, k]
        in_first = (w < 6 * LEAVES_DEV) & (count < BUDGET)

        @pl.when(in_first if part == 1 else jnp.logical_not(in_first))
        def _():
            add_block(i, w, tgt, vals, feats, acc)

        return count + in_first.astype(jnp.int32)

    lax.fori_loop(0, LEAVES_DEV * (NB - 1), item, jnp.int32(0))


def join(mine, theirs, joined):
    n = mine.shape[0]
    joined[:n] = mine[...]
    joined[n:] = theirs[...]


def first_kernel(place, pair, mine, theirs, acc, tgt, vals, feats, joined, tmp):
    join(mine, theirs, joined)
    acc[...] = jnp.zeros_like(acc)
    target_features(pair.at[0], tgt, tmp)
    for slot in range(2):
        load_cluster(pair.at[slot], slot, place[1], vals, feats, tmp)
    own_blocks(0, SELF[0], tgt, vals, feats, acc)


def own_blocks(first, last, tgt, vals, feats, acc):
    def one(i, carry):
        add_block(i, i, tgt, vals, feats, acc)
        return carry

    lax.fori_loop(first, last, one, 0)


def own_kernel(step, acc_in, tgt, vals, feats, mine, theirs, acc, joined):
    join(mine, theirs, joined)
    own_blocks(SELF[step - 1], SELF[step], tgt, vals, feats, acc)


def near_kernel(place, work, near1, near2, tgt, mine, theirs, a_, v_, f_, acc, vals, feats, joined, tmp):
    join(mine, theirs, joined)
    for slot in range(2, 6):
        piece = near1 if slot < 4 else near2
        load_cluster(piece.at[slot % 2], slot, place[1], vals, feats, tmp)
    add_listed(1, work, tgt, vals, feats, acc)


def last_kernel(place, work, far1, far2, tgt, down, basis, a_, v_, f_, acc, vals, feats, out, tmp):
    for slot in range(6, 9):
        block = far1.at[slot - 6] if slot < 8 else far2.at[0]
        load_cluster(block, slot, place[1], vals, feats, tmp)
    add_listed(2, work, tgt, vals, feats, acc)
    scale = 1.0 / math.sqrt(NB * LEAF)
    for l in range(LEAVES_DEV):
        far = lax.dot_general(
            down[...], basis[l], (((1,), (1,)), ((), ())), preferred_element_type=f32
        )
        out[:, l * LEAF : (l + 1) * LEAF] = (acc[l] * scale + far).astype(bf16)


ACC = jax.ShapeDtypeStruct((LEAVES_DEV, RHS, LEAF), f32)
TGT = jax.ShapeDtypeStruct((LEAVES_DEV, FEATS, LEAF), bf16)
VALS = jax.ShapeDtypeStruct((9 * LEAVES_DEV, RHS, LEAF), bf16)
FEAT = jax.ShapeDtypeStruct((9 * LEAVES_DEV, FEATS, LEAF), bf16)
TMP = pltpu.VMEM((LEAVES_DEV, FEATS, LEAF), f32)


def staged(kernel, smem, inputs, state, outs, blocks, scratch=(TMP,)):
    ins = len(smem) + len(inputs)
    state_shapes = [jax.ShapeDtypeStruct(s.shape, s.dtype) for s in state]
    return pl.pallas_call(
        kernel,
        out_shape=tuple(state_shapes) + tuple(outs),
        in_specs=[SM] * len(smem) + [VM] * (len(inputs) + len(state)),
        out_specs=(VM,) * (len(state) + len(outs)),
        scratch_shapes=list(scratch),
        input_output_aliases={ins + n: n for n in range(len(state))},
        compiler_params=params(40),
        cost_estimate=pl.CostEstimate(
            flops=blocks * 10**9, bytes_accessed=10**6, transcendentals=blocks * 10**6
        ),
    )(*smem, *inputs, *state)


def tree_kernel(place, flags, coefs, transfer, coupling, out):
    me = place[0]

    def dot(a, b):
        return jnp.dot(a, b, precision=lax.Precision.HIGHEST, preferred_element_type=f32)

    levels = 4
    cur = [coefs[m] for m in range(32)]
    coupled = []
    for t in range(levels):
        total = jnp.zeros((RHS, RANK), f32)
        for m in range(3):
            flag = flags[t, m].astype(f32)
            total = total + flag * dot(cur[m + 1], coupling[t, m])
        coupled.append(total)
        if t + 1 < levels:
            right = ((me >> t) & 1) == 1
            even = jnp.concatenate(cur[0::2], axis=0)
            odd = jnp.concatenate(cur[1::2], axis=0)
            merged = dot(jnp.where(right, odd, even), transfer[t, 0]) + dot(
                jnp.where(right, even, odd), transfer[t, 1]
            )
            cur = [merged[m * RHS : (m + 1) * RHS] for m in range(len(cur) // 2)]
    local = coupled[-1]
    for t in range(levels - 1, 0, -1):
        right = ((me >> (t - 1)) & 1) == 1
        mat = jnp.where(right, transfer[t - 1, 1], transfer[t - 1, 0])
        local = coupled[t - 1] + lax.dot_general(
            local,
            mat,
            (((1,), (1,)), ((), ())),
            precision=lax.Precision.HIGHEST,
            preferred_element_type=f32,
        )
    out[...] = local.astype(bf16)


def tree(place, flags, coefs, transfer, coupling):
    return pl.pallas_call(
        tree_kernel,
        out_shape=jax.ShapeDtypeStruct((RHS, RANK), bf16),
        in_specs=[SM, SM, VM, VM, VM],
        out_specs=VM,
        compiler_params=params(16),
        cost_estimate=pl.CostEstimate(flops=10**9, bytes_accessed=10**6, transcendentals=0),
    )(place, flags, coefs, transfer, coupling)


def work_list(near_list, me, sign):
    offset = (near_list // LEAVES_DEV - me) * sign
    slot = jnp.zeros_like(offset)
    for n, o in enumerate(SLOT_OFFSETS):
        slot = jnp.where(offset == o, n, slot)
    return slot * LEAVES_DEV + near_list % LEAVES_DEV


def gate_kernel(*refs):
    pass


def gate(array, after):
    anywhere = pl.BlockSpec(memory_space=pl.ANY)
    return pl.pallas_call(
        gate_kernel,
        out_shape=jax.ShapeDtypeStruct(array.shape, array.dtype),
        in_specs=[anywhere, anywhere],
        out_specs=anywhere,
        input_output_aliases={0: 0},
    )(array, after)


def joined_shape(n):
    return jax.ShapeDtypeStruct((n, RHS, RANK), f32)


def partner(coefs, step):
    return permuted(coefs, lambda i: i ^ (1 << step))


def local(charges, points, leaf_basis, transfer, coupling, near_list, couple_flags):
    me = lax.axis_index("leaf")
    sign = 1 - 2 * (me % 2)
    place = jnp.stack([me, sign]).astype(jnp.int32)
    work = work_list(near_list, me, sign)

    own = pack(charges, points)
    sib = permuted(own, lambda i: i ^ 1)
    pair = jnp.stack([own, sib])
    near1 = permuted(pair, lambda i: i - 1 if i % 2 == 0 else i + 1)

    coefs = jnp.dot(
        charges,
        leaf_basis.reshape(LEAVES_DEV * LEAF, RANK),
        preferred_element_type=f32,
    )[None]
    recv = partner(coefs, 0)
    following = partner(jnp.concatenate([coefs, recv]), 1)
    acc, tgt, vals, feats, coefs = staged(
        first_kernel, [place], [pair, coefs, recv], [], [ACC, TGT, VALS, FEAT, joined_shape(2)], 2
    )
    for step in range(1, 4):
        recv = following
        following = partner(jnp.concatenate([coefs, recv]), step + 1)

        def own_step(t, v, f, c, r, a, acc, joined, step=step):
            own_kernel(step, a, t, v, f, c, r, acc, joined)

        acc, coefs = staged(
            own_step,
            [],
            [tgt, vals, feats, coefs, recv],
            [acc],
            [joined_shape(2 ** (step + 1))],
            2,
            (),
        )
        if step == 2:
            near1 = gate(near1, coefs)
            near2 = permuted(near1, lambda i: i ^ 1)
            far1 = permuted(near1, lambda i: i - 2 if i % 2 == 0 else i + 2)
    acc, vals, feats, coefs = staged(
        near_kernel,
        [place, work],
        [near1, near2, tgt, coefs, following],
        [acc, vals, feats],
        [joined_shape(32)],
        BUDGET,
    )
    far1 = gate(far1, coefs)
    far2 = permuted(far1[:1], lambda i: i ^ 1)
    down = tree(place, couple_flags[0], coefs, transfer, coupling)
    return staged(
        last_kernel,
        [place, work],
        [far1, far2, tgt, down, leaf_basis],
        [acc, vals, feats],
        [jax.ShapeDtypeStruct((RHS, LEAVES_DEV * LEAF), bf16)],
        21,
    )[-1]


def solution(mesh):
    return jax.shard_map(
        local,
        mesh=mesh,
        in_specs=(
            P(None, "leaf"),
            P(None, "leaf"),
            P("leaf", None, None),
            P(),
            P(),
            P("leaf", None),
            P("leaf", None, None),
        ),
        out_specs=P(None, "leaf"),
        check_vma=False,
    )
```

```python
import functools
import math

import jax
import jax.numpy as jnp
from jax import lax
from jax.experimental import pallas as pl
from jax.experimental.pallas import tpu as pltpu
from jax.sharding import PartitionSpec as P

bf16 = jnp.bfloat16
f32 = jnp.float32
smoothing_sq = 0.01
LEAF = 1024
HALF = 512
LEAVES_DEV = 8
RHS = 16
RANK = 128
NB = 5
FEATS = 16
PAYLOAD = (19, 16, HALF)
VM = pl.BlockSpec(memory_space=pltpu.VMEM)
SM = pl.BlockSpec(memory_space=pltpu.SMEM)
SLOT_OFFSETS = (0, 1, -1, -2, 2, 3, -3, -4, 4)
SELF = (2, 5, 8)
BUDGET = 11


def params(mib):
    return pltpu.CompilerParams(vmem_limit_bytes=mib * 2**20)


def permuted(array, source_of):
    count = lax.axis_size("leaf")
    route = [(source_of(i), i) for i in range(count) if 0 <= source_of(i) < count]
    return lax.ppermute(array, "leaf", route)


def pack_kernel(charges_hbm, points_hbm, out, charges, points, rows, sems):
    get_points = pltpu.make_async_copy(points_hbm, points, sems.at[0])
    get_charges = pltpu.make_async_copy(charges_hbm, charges, sems.at[1])
    get_points.start()
    get_charges.start()
    get_points.wait()
    for l in range(LEAVES_DEV):
        for h in range(2):
            start = l * LEAF + h * HALF
            part = points[:, start : start + HALF].astype(f32)
            for c in range(3):
                row = h * 24 + c * 8 + l
                rows[row : row + 1, :] = part[c : c + 1]
    for k in range(3):
        out[16 + k] = rows[k * 16 : (k + 1) * 16, :].astype(bf16)
    get_charges.wait()
    for k in range(16):
        out[k] = charges[:, k * HALF : (k + 1) * HALF]


def pack(charges, points):
    anywhere = pl.BlockSpec(memory_space=pl.ANY)
    return pl.pallas_call(
        pack_kernel,
        out_shape=jax.ShapeDtypeStruct(PAYLOAD, bf16),
        in_specs=[anywhere, anywhere],
        out_specs=VM,
        scratch_shapes=[
            pltpu.VMEM(charges.shape, bf16),
            pltpu.VMEM(points.shape, bf16),
            pltpu.VMEM((48, HALF), f32),
            pltpu.SemaphoreType.DMA((2,)),
        ],
        compiler_params=params(4),
        cost_estimate=pl.CostEstimate(flops=10**6, bytes_accessed=10**6, transcendentals=0),
    )(charges, points)


def coordinates(block):
    rows = jnp.concatenate([block[16], block[17], block[18]], axis=0).astype(f32)
    return jnp.concatenate([rows[:24], rows[24:]], axis=1)


def squared_norm_parts(block, first_leaf, extra):
    pts = coordinates(block)
    leaf = lax.broadcasted_iota(jnp.int32, (LEAVES_DEV, LEAF), 0) + first_leaf
    a = leaf.astype(f32) * (1.0 / 64.0)
    x, y, z = pts[0:8], pts[8:16], pts[16:24]
    full_x = x + a
    norm = full_x * full_x + y * y + z * z + extra
    high = norm.astype(bf16).astype(f32)
    rest = norm - high
    middle = rest.astype(bf16).astype(f32)
    return x, a, y, z, high, middle, rest - middle


def store_features(dst, base, rows, tmp):
    for f, row in enumerate(rows):
        tmp[:, f, :] = row
    for f in range(len(rows), FEATS):
        tmp[:, f, :] = jnp.zeros((LEAVES_DEV, LEAF), f32)
    for l in range(LEAVES_DEV):
        dst[base + l] = tmp[l].astype(bf16)


def source_features(block, first_leaf, dst, base, tmp):
    x, a, y, z, high, middle, low = squared_norm_parts(block, first_leaf, 0.0)
    one = jnp.ones_like(x)
    store_features(dst, base, [x, x, a, a, y, z, high, middle, low, one, one, one], tmp)


def target_features(block, dst, tmp):
    x, a, y, z, high, middle, low = squared_norm_parts(block, 0, smoothing_sq)
    one = jnp.ones_like(x)
    rows = [-2 * x, -2 * a, -2 * x, -2 * a, -2 * y, -2 * z, one, one, one, high, middle, low]
    store_features(dst, 0, rows, tmp)


def load_cluster(block, slot, sign, vals, feats, tmp):
    for l in range(LEAVES_DEV):
        vals[slot * LEAVES_DEV + l, :, :HALF] = block[2 * l]
        vals[slot * LEAVES_DEV + l, :, HALF:] = block[2 * l + 1]
    first_leaf = SLOT_OFFSETS[slot] * LEAVES_DEV * sign
    source_features(block, first_leaf, feats, slot * LEAVES_DEV, tmp)


def add_block(i, w, tgt, vals, feats, acc):
    src = feats[w].astype(f32).T.astype(bf16)
    for t in range(0, LEAF, 512):
        dist_sq = jnp.dot(src, tgt[i, :, t : t + 512], preferred_element_type=f32)
        kernel_vals = lax.rsqrt(dist_sq).astype(bf16)
        acc[i, :, t : t + 512] += jnp.dot(vals[w], kernel_vals, preferred_element_type=f32)


def add_listed(part, work, tgt, vals, feats, acc):
    def item(it, count):
        i, k = it // (NB - 1), it % (NB - 1) + 1
        w = work[i, k]
        in_first = (w < 6 * LEAVES_DEV) & (count < BUDGET)

        @pl.when(in_first if part == 1 else jnp.logical_not(in_first))
        def _():
            add_block(i, w, tgt, vals, feats, acc)

        return count + in_first.astype(jnp.int32)

    lax.fori_loop(0, LEAVES_DEV * (NB - 1), item, jnp.int32(0))


def join(mine, theirs, joined):
    n = mine.shape[0]
    joined[:n] = mine[...]
    joined[n:] = theirs[...]


def first_kernel(place, pair, mine, theirs, acc, tgt, vals, feats, joined, tmp):
    join(mine, theirs, joined)
    acc[...] = jnp.zeros_like(acc)
    target_features(pair.at[0], tgt, tmp)
    for slot in range(2):
        load_cluster(pair.at[slot], slot, place[1], vals, feats, tmp)
    own_blocks(0, SELF[0], tgt, vals, feats, acc)


def own_blocks(first, last, tgt, vals, feats, acc):
    def one(i, carry):
        add_block(i, i, tgt, vals, feats, acc)
        return carry

    lax.fori_loop(first, last, one, 0)


def own_kernel(step, acc_in, tgt, vals, feats, mine, theirs, acc, joined):
    join(mine, theirs, joined)
    own_blocks(SELF[step - 1], SELF[step], tgt, vals, feats, acc)


def near_kernel(place, work, near1, near2, tgt, mine, theirs, a_, v_, f_, acc, vals, feats, joined, tmp):
    join(mine, theirs, joined)
    for slot in range(2, 6):
        piece = near1 if slot < 4 else near2
        load_cluster(piece.at[slot % 2], slot, place[1], vals, feats, tmp)
    add_listed(1, work, tgt, vals, feats, acc)


def tree_kernel(
    place, flags, far1, mine, theirs, transfer, coupling, v_, f_, vals, feats, down, tmp
):
    for slot in range(6, 8):
        load_cluster(far1.at[slot - 6], slot, place[1], vals, feats, tmp)
    n = mine.shape[0]
    coefs = [mine[m] for m in range(n)] + [theirs[m] for m in range(n)]
    down[...] = tree(place[0], flags, coefs, transfer, coupling)


def last_kernel(place, work, far2, tgt, down, basis, a_, v_, f_, acc, vals, feats, out, tmp):
    load_cluster(far2.at[0], 8, place[1], vals, feats, tmp)
    add_listed(2, work, tgt, vals, feats, acc)
    scale = 1.0 / math.sqrt(NB * LEAF)
    for l in range(LEAVES_DEV):
        far = lax.dot_general(
            down[...], basis[l], (((1,), (1,)), ((), ())), preferred_element_type=f32
        )
        out[:, l * LEAF : (l + 1) * LEAF] = (acc[l] * scale + far).astype(bf16)


ACC = jax.ShapeDtypeStruct((LEAVES_DEV, RHS, LEAF), f32)
TGT = jax.ShapeDtypeStruct((LEAVES_DEV, FEATS, LEAF), bf16)
VALS = jax.ShapeDtypeStruct((9 * LEAVES_DEV, RHS, LEAF), bf16)
FEAT = jax.ShapeDtypeStruct((9 * LEAVES_DEV, FEATS, LEAF), bf16)
TMP = pltpu.VMEM((LEAVES_DEV, FEATS, LEAF), f32)


def staged(kernel, smem, inputs, state, outs, blocks, scratch=(TMP,)):
    ins = len(smem) + len(inputs)
    state_shapes = [jax.ShapeDtypeStruct(s.shape, s.dtype) for s in state]
    return pl.pallas_call(
        kernel,
        out_shape=tuple(state_shapes) + tuple(outs),
        in_specs=[SM] * len(smem) + [VM] * (len(inputs) + len(state)),
        out_specs=(VM,) * (len(state) + len(outs)),
        scratch_shapes=list(scratch),
        input_output_aliases={ins + n: n for n in range(len(state))},
        compiler_params=params(16),
        cost_estimate=pl.CostEstimate(
            flops=blocks * 10**9, bytes_accessed=10**6, transcendentals=blocks * 10**6
        ),
    )(*smem, *inputs, *state)


def tree(me, flags, coefs, transfer, coupling):
    def dot(a, b):
        return jnp.dot(a, b, precision=lax.Precision.HIGHEST, preferred_element_type=f32)

    levels = 4
    cur = coefs
    coupled = []
    for t in range(levels):
        total = jnp.zeros((RHS, RANK), f32)
        for m in range(3):
            flag = flags[t, m].astype(f32)
            total = total + flag * dot(cur[m + 1], coupling[t, m])
        coupled.append(total)
        if t + 1 < levels:
            right = ((me >> t) & 1) == 1
            even = jnp.concatenate(cur[0::2], axis=0)
            odd = jnp.concatenate(cur[1::2], axis=0)
            merged = dot(jnp.where(right, odd, even), transfer[t, 0]) + dot(
                jnp.where(right, even, odd), transfer[t, 1]
            )
            cur = [merged[m * RHS : (m + 1) * RHS] for m in range(len(cur) // 2)]
    local = coupled[-1]
    for t in range(levels - 1, 0, -1):
        right = ((me >> (t - 1)) & 1) == 1
        mat = jnp.where(right, transfer[t - 1, 1], transfer[t - 1, 0])
        local = coupled[t - 1] + lax.dot_general(
            local,
            mat,
            (((1,), (1,)), ((), ())),
            precision=lax.Precision.HIGHEST,
            preferred_element_type=f32,
        )
    return local.astype(bf16)


def work_list(near_list, me, sign):
    offset = (near_list // LEAVES_DEV - me) * sign
    slot = jnp.zeros_like(offset)
    for n, o in enumerate(SLOT_OFFSETS):
        slot = jnp.where(offset == o, n, slot)
    return slot * LEAVES_DEV + near_list % LEAVES_DEV


def gate_kernel(*refs):
    pass


def gate(array, after):
    return pl.pallas_call(
        gate_kernel,
        out_shape=jax.ShapeDtypeStruct(array.shape, array.dtype),
        in_specs=[VM, VM],
        out_specs=VM,
        input_output_aliases={0: 0},
        compiler_params=params(2),
    )(array, after)


def gate_copy_kernel(array, after, out):
    out[0] = array[0]


def gate_first(array, after):
    return pl.pallas_call(
        gate_copy_kernel,
        out_shape=jax.ShapeDtypeStruct((1,) + array.shape[1:], array.dtype),
        in_specs=[VM, VM],
        out_specs=VM,
        compiler_params=params(2),
    )(array, after)


def joined_shape(n):
    return jax.ShapeDtypeStruct((n, RHS, RANK), f32)


def partner(coefs, step):
    return permuted(coefs, lambda i: i ^ (1 << step))


def local(charges, points, leaf_basis, transfer, coupling, near_list, couple_flags):
    me = lax.axis_index("leaf")
    sign = 1 - 2 * (me % 2)
    place = jnp.stack([me, sign]).astype(jnp.int32)
    work = work_list(near_list, me, sign)

    own = pack(charges, points)
    sib = permuted(own, lambda i: i ^ 1)
    pair = jnp.stack([own, sib])
    near1 = permuted(pair, lambda i: i - 1 if i % 2 == 0 else i + 1)

    coefs = jnp.dot(
        charges,
        leaf_basis.reshape(LEAVES_DEV * LEAF, RANK),
        preferred_element_type=f32,
    )[None]
    recv = partner(coefs, 0)
    following = partner(jnp.concatenate([coefs, recv]), 1)
    acc, tgt, vals, feats, coefs = staged(
        first_kernel, [place], [pair, coefs, recv], [], [ACC, TGT, VALS, FEAT, joined_shape(2)], 2
    )
    for step in range(1, 3):
        recv = following
        following = partner(jnp.concatenate([coefs, recv]), step + 1)

        def own_step(t, v, f, c, r, a, acc, joined, step=step):
            own_kernel(step, a, t, v, f, c, r, acc, joined)

        acc, coefs = staged(
            own_step,
            [],
            [tgt, vals, feats, coefs, recv],
            [acc],
            [joined_shape(2 ** (step + 1))],
            3,
            (),
        )
        if step == 1:
            near1 = gate(near1, coefs)
            near2 = permuted(near1, lambda i: i ^ 1)
            far1 = permuted(near1, lambda i: i - 2 if i % 2 == 0 else i + 2)
    recv = following
    following = partner(jnp.concatenate([coefs, recv]), 4)
    acc, vals, feats, coefs = staged(
        near_kernel,
        [place, work],
        [near1, near2, tgt, coefs, recv],
        [acc, vals, feats],
        [joined_shape(16)],
        BUDGET,
    )
    far2 = permuted(gate_first(far1, coefs), lambda i: i ^ 1)
    vals, feats, down = staged(
        tree_kernel,
        [place, couple_flags[0]],
        [far1, coefs, following, transfer, coupling],
        [vals, feats],
        [jax.ShapeDtypeStruct((RHS, RANK), bf16)],
        3,
    )
    return staged(
        last_kernel,
        [place, work],
        [far2, tgt, down, leaf_basis],
        [acc, vals, feats],
        [jax.ShapeDtypeStruct((RHS, LEAVES_DEV * LEAF), bf16)],
        21,
    )[-1]


def solution(mesh):
    return jax.shard_map(
        local,
        mesh=mesh,
        in_specs=(
            P(None, "leaf"),
            P(None, "leaf"),
            P("leaf", None, None),
            P(),
            P(),
            P("leaf", None),
            P("leaf", None, None),
        ),
        out_specs=P(None, "leaf"),
        check_vma=False,
    )
```

```python
import functools
import math

import jax
import jax.numpy as jnp
from jax import lax
from jax.experimental import pallas as pl
from jax.experimental.pallas import tpu as pltpu
from jax.sharding import PartitionSpec as P

bf16 = jnp.bfloat16
f32 = jnp.float32
smoothing_sq = 0.01
LEAF = 1024
HALF = 512
LEAVES_DEV = 8
RHS = 16
RANK = 128
NB = 5
FEATS = 16
PAYLOAD = (19, 16, HALF)
VM = pl.BlockSpec(memory_space=pltpu.VMEM)
SM = pl.BlockSpec(memory_space=pltpu.SMEM)
SLOT_OFFSETS = (0, 1, -1, -2, 2, 3, -3, -4, 4)
SELF = (1, 2, 8)
BITS = (0, 3, 4, 1, 2)
BUDGET = 11


def params(mib):
    return pltpu.CompilerParams(vmem_limit_bytes=mib * 2**20)


def permuted(array, source_of):
    count = lax.axis_size("leaf")
    route = [(source_of(i), i) for i in range(count) if 0 <= source_of(i) < count]
    return lax.ppermute(array, "leaf", route)


def pack_kernel(charges_hbm, points_hbm, out, charges, points, rows, sems):
    get_points = pltpu.make_async_copy(points_hbm, points, sems.at[0])
    get_charges = pltpu.make_async_copy(charges_hbm, charges, sems.at[1])
    get_points.start()
    get_charges.start()
    get_points.wait()
    for l in range(LEAVES_DEV):
        for h in range(2):
            start = l * LEAF + h * HALF
            part = points[:, start : start + HALF].astype(f32)
            for c in range(3):
                row = h * 24 + c * 8 + l
                rows[row : row + 1, :] = part[c : c + 1]
    for k in range(3):
        out[16 + k] = rows[k * 16 : (k + 1) * 16, :].astype(bf16)
    get_charges.wait()
    for k in range(16):
        out[k] = charges[:, k * HALF : (k + 1) * HALF]


def pack(charges, points):
    anywhere = pl.BlockSpec(memory_space=pl.ANY)
    return pl.pallas_call(
        pack_kernel,
        out_shape=jax.ShapeDtypeStruct(PAYLOAD, bf16),
        in_specs=[anywhere] * 2,
        out_specs=VM,
        scratch_shapes=[
            pltpu.VMEM(charges.shape, bf16),
            pltpu.VMEM(points.shape, bf16),
            pltpu.VMEM((48, HALF), f32),
            pltpu.SemaphoreType.DMA((2,)),
        ],
        compiler_params=params(60),
        cost_estimate=pl.CostEstimate(flops=10**6, bytes_accessed=10**6, transcendentals=0),
    )(charges, points)


def coordinates(block):
    rows = jnp.concatenate([block[16], block[17], block[18]], axis=0).astype(f32)
    return jnp.concatenate([rows[:24], rows[24:]], axis=1)


def squared_norm_parts(block, first_leaf, extra):
    pts = coordinates(block)
    leaf = lax.broadcasted_iota(jnp.int32, (LEAVES_DEV, LEAF), 0) + first_leaf
    a = leaf.astype(f32) * (1.0 / 64.0)
    x, y, z = pts[0:8], pts[8:16], pts[16:24]
    full_x = x + a
    norm = full_x * full_x + y * y + z * z + extra
    high = norm.astype(bf16).astype(f32)
    rest = norm - high
    middle = rest.astype(bf16).astype(f32)
    return x, a, y, z, high, middle, rest - middle


def store_features(dst, base, rows, tmp):
    for f, row in rows:
        tmp[:, f, :] = row
    for l in range(LEAVES_DEV):
        dst[base + l] = tmp[l].astype(bf16)


def constant_rows(tmp, ones):
    for f in range(FEATS):
        if f in ones:
            tmp[:, f, :] = jnp.ones((LEAVES_DEV, LEAF), f32)
        elif f >= 12:
            tmp[:, f, :] = jnp.zeros((LEAVES_DEV, LEAF), f32)


def source_features(block, first_leaf, dst, base, tmp):
    x, a, y, z, high, middle, low = squared_norm_parts(block, first_leaf, 0.0)
    store_features(dst, base, list(enumerate([x, x, a, a, y, z, high, middle, low])), tmp)


def target_features(block, dst, tmp):
    x, a, y, z, high, middle, low = squared_norm_parts(block, 0, smoothing_sq)
    rows = list(enumerate([-2 * x, -2 * a, -2 * x, -2 * a, -2 * y, -2 * z]))
    store_features(dst, 0, rows + [(9, high), (10, middle), (11, low)], tmp)


def load_cluster(block, slot, sign, vals, feats, tmp):
    for l in range(LEAVES_DEV):
        vals[slot * LEAVES_DEV + l, :, :HALF] = block[2 * l]
        vals[slot * LEAVES_DEV + l, :, HALF:] = block[2 * l + 1]
    first_leaf = SLOT_OFFSETS[slot] * LEAVES_DEV * sign
    source_features(block, first_leaf, feats, slot * LEAVES_DEV, tmp)


def add_block(i, w, tgt, vals, feats, acc):
    src = feats[w].astype(f32).T.astype(bf16)
    for t in range(0, LEAF, 512):
        dist_sq = jnp.dot(src, tgt[i, :, t : t + 512], preferred_element_type=f32)
        kernel_vals = lax.rsqrt(dist_sq).astype(bf16)
        acc[i, :, t : t + 512] += jnp.dot(vals[w], kernel_vals, preferred_element_type=f32)


def add_listed(part, work, tgt, vals, feats, acc):
    def item(it, count):
        i, k = it // (NB - 1), it % (NB - 1) + 1
        w = work[i, k]
        in_first = (w < 6 * LEAVES_DEV) & (count < BUDGET)

        @pl.when(in_first if part == 1 else jnp.logical_not(in_first))
        def _():
            add_block(i, w, tgt, vals, feats, acc)

        return count + in_first.astype(jnp.int32)

    lax.fori_loop(0, LEAVES_DEV * (NB - 1), item, jnp.int32(0))


def own_blocks(first, last, tgt, vals, feats, acc):
    def one(i, carry):
        add_block(i, i, tgt, vals, feats, acc)
        return carry

    lax.fori_loop(first, last, one, 0)


def join(mine, theirs, joined):
    n = mine.shape[0]
    joined[:n] = mine[...]
    joined[n:] = theirs[...]


def first_kernel(place, own, mine, theirs, acc, tgt, vals, feats, joined, tmp):
    join(mine, theirs, joined)
    acc[...] = jnp.zeros_like(acc)
    constant_rows(tmp, (6, 7, 8))
    target_features(own, tgt, tmp)
    constant_rows(tmp, (9, 10, 11))
    load_cluster(own, 0, place[1], vals, feats, tmp)
    own_blocks(0, SELF[0], tgt, vals, feats, acc)


def own_kernel(step, tgt, vals, feats, mine, theirs, acc_in, acc, joined):
    join(mine, theirs, joined)
    own_blocks(SELF[step - 1], SELF[step], tgt, vals, feats, acc)


def load_clusters(pieces, sign, vals, feats, tmp):
    constant_rows(tmp, (9, 10, 11))
    slot = 0
    for piece in pieces:
        for part in range(piece.shape[0]):
            load_cluster(piece.at[part], slot, sign, vals, feats, tmp)
            slot += 1


def near_kernel(
    place, work, pair, near1, near2, mine, theirs, acc_in, acc, joined, vals, feats, tmp, tgt
):
    join(mine, theirs, joined)
    constant_rows(tmp, (6, 7, 8))
    target_features(pair.at[0], tgt, tmp)
    load_clusters([pair, near1, near2], place[1], vals, feats, tmp)
    add_listed(1, work, tgt, vals, feats, acc)


def last_kernel(place, work, pair, near1, near2, far1, far2, acc_in, acc, vals, feats, tmp, tgt):
    constant_rows(tmp, (6, 7, 8))
    target_features(pair.at[0], tgt, tmp)
    load_clusters([pair, near1, near2, far1, far2], place[1], vals, feats, tmp)
    add_listed(2, work, tgt, vals, feats, acc)


def tree_kernel(place, flags, acc, *refs):
    groups, (transfer, coupling, basis, out) = refs[:2], refs[2:]
    coefs = []
    for m in range(32):
        where = sum(((m >> bit) & 1) << at for at, bit in enumerate(BITS))
        coefs.append(groups[where // 16][where % 16])
    down = tree(place[0], flags, coefs, transfer, coupling)
    scale = 1.0 / math.sqrt(NB * LEAF)
    for l in range(LEAVES_DEV):
        far = lax.dot_general(
            down, basis[l], (((1,), (1,)), ((), ())), preferred_element_type=f32
        )
        out[:, l * LEAF : (l + 1) * LEAF] = (acc[l] * scale + far).astype(bf16)


ACC = jax.ShapeDtypeStruct((LEAVES_DEV, RHS, LEAF), f32)
TMP = pltpu.VMEM((LEAVES_DEV, FEATS, LEAF), f32)


def window_scratch(slots):
    return (
        pltpu.VMEM((slots * LEAVES_DEV, RHS, LEAF), bf16),
        pltpu.VMEM((slots * LEAVES_DEV, FEATS, LEAF), bf16),
        TMP,
        pltpu.VMEM((LEAVES_DEV, FEATS, LEAF), bf16),
    )


TGT = jax.ShapeDtypeStruct((LEAVES_DEV, FEATS, LEAF), bf16)
VALS = jax.ShapeDtypeStruct((LEAVES_DEV, RHS, LEAF), bf16)


def staged(kernel, smem, inputs, state, outs, blocks, scratch=(), unplaced=0):
    ins = len(smem) + len(inputs)
    state_shapes = [jax.ShapeDtypeStruct(s.shape, s.dtype) for s in state]
    return pl.pallas_call(
        kernel,
        out_shape=tuple(state_shapes) + tuple(outs),
        in_specs=[SM] * len(smem)
        + [VM] * (len(inputs) - unplaced)
        + [pl.BlockSpec(memory_space=pl.ANY)] * unplaced
        + [VM] * len(state),
        out_specs=(VM,) * (len(state) + len(outs)),
        scratch_shapes=list(scratch),
        input_output_aliases={ins + n: n for n in range(len(state))},
        compiler_params=params(16),
        cost_estimate=pl.CostEstimate(
            flops=blocks * 10**9, bytes_accessed=10**6, transcendentals=blocks * 10**6
        ),
    )(*smem, *inputs, *state)


def tree(me, flags, coefs, transfer, coupling):
    def dot(a, b):
        return jnp.dot(a, b, precision=lax.Precision.HIGHEST, preferred_element_type=f32)

    levels = 4
    cur = coefs
    coupled = []
    for t in range(levels):
        chosen = [flags[t, m].astype(f32) * cur[m + 1] for m in range(3)]
        coupled.append(
            dot(jnp.concatenate(chosen, axis=1), coupling[t].reshape(3 * RANK, RANK))
        )
        if t + 1 < levels:
            right = ((me >> t) & 1) == 1
            even = jnp.concatenate(cur[0::2], axis=0)
            odd = jnp.concatenate(cur[1::2], axis=0)
            both = jnp.concatenate(
                [jnp.where(right, odd, even), jnp.where(right, even, odd)], axis=1
            )
            merged = dot(both, transfer[t].reshape(2 * RANK, RANK))
            cur = [merged[m * RHS : (m + 1) * RHS] for m in range(len(cur) // 2)]
    local = coupled[-1]
    for t in range(levels - 1, 0, -1):
        right = ((me >> (t - 1)) & 1) == 1
        mat = jnp.where(right, transfer[t - 1, 1], transfer[t - 1, 0])
        local = coupled[t - 1] + lax.dot_general(
            local,
            mat,
            (((1,), (1,)), ((), ())),
            precision=lax.Precision.HIGHEST,
            preferred_element_type=f32,
        )
    return local.astype(bf16)


def work_list(near_list, me, sign):
    offset = (near_list // LEAVES_DEV - me) * sign
    slot = jnp.zeros_like(offset)
    for n, o in enumerate(SLOT_OFFSETS):
        slot = jnp.where(offset == o, n, slot)
    return slot * LEAVES_DEV + near_list % LEAVES_DEV


def gate_kernel(*refs):
    pass


def gate(array, *after):
    return pl.pallas_call(
        gate_kernel,
        out_shape=jax.ShapeDtypeStruct(array.shape, array.dtype),
        in_specs=[VM] * (1 + len(after)),
        out_specs=VM,
        input_output_aliases={0: 0},
        compiler_params=params(2),
    )(array, *after)


def gate_copy_kernel(array, *refs):
    refs[-1][0] = array[0]


def gate_first(array, *after):
    return pl.pallas_call(
        gate_copy_kernel,
        out_shape=jax.ShapeDtypeStruct((1,) + array.shape[1:], array.dtype),
        in_specs=[VM] * (1 + len(after)),
        out_specs=VM,
        compiler_params=params(2),
    )(array, *after)


def partner(coefs, step):
    return permuted(coefs, lambda i: i ^ (1 << BITS[step]))


def joined_shape(n):
    return jax.ShapeDtypeStruct((n, RHS, RANK), f32)


def local(charges, points, leaf_basis, transfer, coupling, near_list, couple_flags):
    me = lax.axis_index("leaf")
    sign = 1 - 2 * (me % 2)
    place = jnp.stack([me, sign]).astype(jnp.int32)
    work = work_list(near_list, me, sign)

    own = pack(charges, points)
    sib = permuted(own, lambda i: i ^ 1)
    pair = jnp.stack([own, sib])
    coefs = jnp.dot(
        charges,
        leaf_basis.reshape(LEAVES_DEV * LEAF, RANK),
        preferred_element_type=f32,
    )[None]
    recv = partner(coefs, 0)
    following = partner(jnp.concatenate([coefs, recv]), 1)
    acc, tgt, vals, feats, coefs = staged(
        first_kernel,
        [place],
        [own, coefs, recv],
        [],
        [ACC, TGT, VALS, TGT, joined_shape(2)],
        2,
        (TMP,),
    )
    for step in (1, 2):
        recv = following
        following = partner(jnp.concatenate([coefs, recv]), step + 1)
        if step == 2:
            pair = gate(pair, recv)
            near1 = permuted(pair, lambda i: i - 1 if i % 2 == 0 else i + 1)
        acc, coefs = staged(
            functools.partial(own_kernel, step),
            [],
            [tgt, vals, feats, coefs, recv],
            [acc],
            [joined_shape(2 ** (step + 1))],
            SELF[step] - SELF[step - 1],
        )
    recv = following
    near1 = gate(near1, acc, recv)
    near2 = permuted(near1, lambda i: i ^ 1)
    far1 = permuted(near1, lambda i: i - 2 if i % 2 == 0 else i + 2)
    following = partner(jnp.concatenate([coefs, recv]), 4)
    acc, coefs = staged(
        near_kernel,
        [place, work],
        [pair, near1, near2, coefs, recv],
        [acc],
        [joined_shape(16)],
        BUDGET,
        window_scratch(6),
    )
    far2 = permuted(gate_first(far1, acc, following), lambda i: i ^ 1)
    (acc,) = staged(
        last_kernel,
        [place, work],
        [pair, near1, near2, far1, far2],
        [acc],
        [],
        21,
        window_scratch(9),
    )
    return staged(
        tree_kernel,
        [place, couple_flags[0]],
        [acc, coefs, following, transfer, coupling, leaf_basis],
        [],
        [jax.ShapeDtypeStruct((RHS, LEAVES_DEV * LEAF), bf16)],
        3,
    )[-1]


def solution(mesh):
    return jax.shard_map(
        local,
        mesh=mesh,
        in_specs=(
            P(None, "leaf"),
            P(None, "leaf"),
            P("leaf", None, None),
            P(),
            P(),
            P("leaf", None),
            P("leaf", None, None),
        ),
        out_specs=P(None, "leaf"),
        check_vma=False,
    )
```

```python
import functools
import math

import jax
import jax.numpy as jnp
from jax import lax
from jax.experimental import pallas as pl
from jax.experimental.pallas import tpu as pltpu
from jax.sharding import PartitionSpec as P

bf16 = jnp.bfloat16
f32 = jnp.float32
smoothing_sq = 0.01
LEAF = 1024
HALF = 512
LEAVES_DEV = 8
RHS = 16
RANK = 128
NB = 5
FEATS = 16
PAYLOAD = (19, 16, HALF)
VM = pl.BlockSpec(memory_space=pltpu.VMEM)
SM = pl.BlockSpec(memory_space=pltpu.SMEM)
SLOT_OFFSETS = (0, 1, -1, -2, 2, 3, -3, -4, 4)
SELF = (1, 2, 8)
BITS = (0, 3, 4, 1, 2)
BUDGET = 12


def params(mib):
    return pltpu.CompilerParams(vmem_limit_bytes=mib * 2**20)


def permuted(array, source_of):
    count = lax.axis_size("leaf")
    route = [(source_of(i), i) for i in range(count) if 0 <= source_of(i) < count]
    return lax.ppermute(array, "leaf", route)


def pack_kernel(charges_hbm, points_hbm, out, charges, points, rows, sems):
    get_points = pltpu.make_async_copy(points_hbm, points, sems.at[0])
    get_charges = pltpu.make_async_copy(charges_hbm, charges, sems.at[1])
    get_points.start()
    get_charges.start()
    get_points.wait()
    for l in range(LEAVES_DEV):
        for h in range(2):
            start = l * LEAF + h * HALF
            part = points[:, start : start + HALF].astype(f32)
            for c in range(3):
                row = h * 24 + c * 8 + l
                rows[row : row + 1, :] = part[c : c + 1]
    for k in range(3):
        out[16 + k] = rows[k * 16 : (k + 1) * 16, :].astype(bf16)
    get_charges.wait()
    for k in range(16):
        out[k] = charges[:, k * HALF : (k + 1) * HALF]


def pack(charges, points):
    anywhere = pl.BlockSpec(memory_space=pl.ANY)
    return pl.pallas_call(
        pack_kernel,
        out_shape=jax.ShapeDtypeStruct(PAYLOAD, bf16),
        in_specs=[anywhere] * 2,
        out_specs=VM,
        scratch_shapes=[
            pltpu.VMEM(charges.shape, bf16),
            pltpu.VMEM(points.shape, bf16),
            pltpu.VMEM((48, HALF), f32),
            pltpu.SemaphoreType.DMA((2,)),
        ],
        compiler_params=params(60),
        cost_estimate=pl.CostEstimate(flops=10**6, bytes_accessed=10**6, transcendentals=0),
    )(charges, points)


def coordinates(block):
    rows = jnp.concatenate([block[16], block[17], block[18]], axis=0).astype(f32)
    return jnp.concatenate([rows[:24], rows[24:]], axis=1)


def squared_norm_parts(block, first_leaf, extra):
    pts = coordinates(block)
    leaf = lax.broadcasted_iota(jnp.int32, (LEAVES_DEV, LEAF), 0) + first_leaf
    a = leaf.astype(f32) * (1.0 / 64.0)
    x, y, z = pts[0:8], pts[8:16], pts[16:24]
    full_x = x + a
    norm = full_x * full_x + y * y + z * z + extra
    high = norm.astype(bf16).astype(f32)
    rest = norm - high
    middle = rest.astype(bf16).astype(f32)
    return x, a, y, z, high, middle, rest - middle


def store_features(dst, base, rows, tmp):
    for f, row in rows:
        tmp[:, f, :] = row
    for l in range(LEAVES_DEV):
        dst[base + l] = tmp[l].astype(bf16)


def constant_rows(tmp, ones):
    for f in range(FEATS):
        if f in ones:
            tmp[:, f, :] = jnp.ones((LEAVES_DEV, LEAF), f32)
        elif f >= 12:
            tmp[:, f, :] = jnp.zeros((LEAVES_DEV, LEAF), f32)


def source_features(block, first_leaf, dst, base, tmp):
    x, a, y, z, high, middle, low = squared_norm_parts(block, first_leaf, 0.0)
    store_features(dst, base, list(enumerate([x, x, a, a, y, z, high, middle, low])), tmp)


def target_features(block, dst, tmp):
    x, a, y, z, high, middle, low = squared_norm_parts(block, 0, smoothing_sq)
    rows = list(enumerate([-2 * x, -2 * a, -2 * x, -2 * a, -2 * y, -2 * z]))
    store_features(dst, 0, rows + [(9, high), (10, middle), (11, low)], tmp)


def load_cluster(block, slot, sign, vals, feats, tmp, window_slot=None):
    for l in range(LEAVES_DEV):
        vals[slot * LEAVES_DEV + l, :, :HALF] = block[2 * l]
        vals[slot * LEAVES_DEV + l, :, HALF:] = block[2 * l + 1]
    offset = SLOT_OFFSETS[slot if window_slot is None else window_slot]
    first_leaf = offset * LEAVES_DEV * sign
    source_features(block, first_leaf, feats, slot * LEAVES_DEV, tmp)


def add_block(i, w, tgt, vals, feats, acc):
    src = feats[w].astype(f32).T.astype(bf16)
    for t in range(0, LEAF, 512):
        dist_sq = jnp.dot(src, tgt[i, :, t : t + 512], preferred_element_type=f32)
        kernel_vals = lax.rsqrt(dist_sq).astype(bf16)
        acc[i, :, t : t + 512] += jnp.dot(vals[w], kernel_vals, preferred_element_type=f32)


def add_listed(part, work, items, tgt, vals, feats, acc):
    def select(it, counts):
        first, chosen = counts
        i, k = it // (NB - 1), it % (NB - 1) + 1
        w = work[i, k]
        in_first = (w < 6 * LEAVES_DEV) & (first < BUDGET)
        in_last = w >= 8 * LEAVES_DEV
        in_part = (
            in_first,
            jnp.logical_not(in_first | in_last),
            in_last,
        )[part - 1]
        items[chosen] = i * 128 + w
        return first + in_first.astype(jnp.int32), chosen + in_part.astype(jnp.int32)

    _, count = lax.fori_loop(
        0, LEAVES_DEV * (NB - 1), select, (jnp.int32(0), jnp.int32(0))
    )
    base = 8 * LEAVES_DEV if part == 3 else 0

    def several(group):
        def some(g, carry):
            for u in range(group):
                item = items[g * group + u]
                add_block(item // 128, item % 128 - base, tgt, vals, feats, acc)
            return carry

        return some

    whole = count // 4
    lax.fori_loop(0, whole, several(4), 0)
    lax.fori_loop(whole * 4, count, several(1), 0)


def own_blocks(first, last, tgt, vals, feats, acc):
    group = 2 if (last - first) % 2 == 0 else 1

    def some(n, carry):
        for u in range(group):
            i = first + n * group + u
            add_block(i, i, tgt, vals, feats, acc)
        return carry

    lax.fori_loop(0, (last - first) // group, some, 0)


def join(mine, theirs, joined):
    n = mine.shape[0]
    joined[:n] = mine[...]
    joined[n:] = theirs[...]


def first_kernel(place, own, mine, theirs, acc, tgt, vals, feats, joined, tmp):
    join(mine, theirs, joined)
    acc[...] = jnp.zeros_like(acc)
    constant_rows(tmp, (6, 7, 8))
    target_features(own, tgt, tmp)
    constant_rows(tmp, (9, 10, 11))
    load_cluster(own, 0, place[1], vals, feats, tmp)
    own_blocks(0, SELF[0], tgt, vals, feats, acc)


def own_kernel(step, tgt, vals, feats, mine, theirs, acc_in, acc, joined):
    join(mine, theirs, joined)
    own_blocks(SELF[step - 1], SELF[step], tgt, vals, feats, acc)


def load_clusters(pieces, sign, vals, feats, tmp):
    constant_rows(tmp, (9, 10, 11))
    slot = 0
    for piece in pieces:
        for part in range(piece.shape[0]):
            load_cluster(piece.at[part], slot, sign, vals, feats, tmp)
            slot += 1


def near_kernel(
    place, work, pair, near1, near2, mine, theirs, acc_in, acc, joined, vals, feats, tmp, tgt, items
):
    join(mine, theirs, joined)
    constant_rows(tmp, (6, 7, 8))
    target_features(pair.at[0], tgt, tmp)
    load_clusters([pair, near1, near2], place[1], vals, feats, tmp)
    add_listed(1, work, items, tgt, vals, feats, acc)


def last_kernel(place, work, pair, near1, near2, far1, acc_in, acc, vals, feats, tmp, tgt, items):
    constant_rows(tmp, (6, 7, 8))
    target_features(pair.at[0], tgt, tmp)
    load_clusters([pair, near1, near2, far1], place[1], vals, feats, tmp)
    add_listed(2, work, items, tgt, vals, feats, acc)


def tree_kernel(
    place, work, flags, pair, far2, mine, theirs, transfer, coupling, basis, acc_in,
    acc, out, vals, feats, tmp, tgt, items,
):
    constant_rows(tmp, (6, 7, 8))
    target_features(pair.at[0], tgt, tmp)
    constant_rows(tmp, (9, 10, 11))
    load_cluster(far2.at[0], 0, place[1], vals, feats, tmp, 8)
    add_listed(3, work, items, tgt, vals, feats, acc)
    n = mine.shape[0]
    coefs = []
    for m in range(2 * n):
        where = sum(((m >> bit) & 1) << at for at, bit in enumerate(BITS))
        coefs.append(mine[where] if where < n else theirs[where - n])
    down = tree(place[0], flags, coefs, transfer, coupling)
    scale = 1.0 / math.sqrt(NB * LEAF)
    for l in range(LEAVES_DEV):
        far = lax.dot_general(
            down, basis[l], (((1,), (1,)), ((), ())), preferred_element_type=f32
        )
        out[:, l * LEAF : (l + 1) * LEAF] = (acc[l] * scale + far).astype(bf16)


ACC = jax.ShapeDtypeStruct((LEAVES_DEV, RHS, LEAF), f32)
TMP = pltpu.VMEM((LEAVES_DEV, FEATS, LEAF), f32)


def window_scratch(slots):
    return (
        pltpu.VMEM((slots * LEAVES_DEV, RHS, LEAF), bf16),
        pltpu.VMEM((slots * LEAVES_DEV, FEATS, LEAF), bf16),
        TMP,
        pltpu.VMEM((LEAVES_DEV, FEATS, LEAF), bf16),
        pltpu.SMEM((LEAVES_DEV * NB,), jnp.int32),
    )


TGT = jax.ShapeDtypeStruct((LEAVES_DEV, FEATS, LEAF), bf16)
VALS = jax.ShapeDtypeStruct((LEAVES_DEV, RHS, LEAF), bf16)


def staged(kernel, smem, inputs, state, outs, blocks, scratch=(), unplaced=0):
    ins = len(smem) + len(inputs)
    state_shapes = [jax.ShapeDtypeStruct(s.shape, s.dtype) for s in state]
    return pl.pallas_call(
        kernel,
        out_shape=tuple(state_shapes) + tuple(outs),
        in_specs=[SM] * len(smem)
        + [VM] * (len(inputs) - unplaced)
        + [pl.BlockSpec(memory_space=pl.ANY)] * unplaced
        + [VM] * len(state),
        out_specs=(VM,) * (len(state) + len(outs)),
        scratch_shapes=list(scratch),
        input_output_aliases={ins + n: n for n in range(len(state))},
        compiler_params=params(16),
        cost_estimate=pl.CostEstimate(
            flops=blocks * 10**9, bytes_accessed=10**6, transcendentals=blocks * 10**6
        ),
    )(*smem, *inputs, *state)


def tree(me, flags, coefs, transfer, coupling):
    def dot(a, b):
        return jnp.dot(a, b, precision=lax.Precision.HIGHEST, preferred_element_type=f32)

    levels = 4
    cur = coefs
    coupled = []
    for t in range(levels):
        chosen = [flags[t, m].astype(f32) * cur[m + 1] for m in range(3)]
        coupled.append(
            dot(jnp.concatenate(chosen, axis=1), coupling[t].reshape(3 * RANK, RANK))
        )
        if t + 1 < levels:
            right = ((me >> t) & 1) == 1
            even = jnp.concatenate(cur[0::2], axis=0)
            odd = jnp.concatenate(cur[1::2], axis=0)
            both = jnp.concatenate(
                [jnp.where(right, odd, even), jnp.where(right, even, odd)], axis=1
            )
            merged = dot(both, transfer[t].reshape(2 * RANK, RANK))
            cur = [merged[m * RHS : (m + 1) * RHS] for m in range(len(cur) // 2)]
    local = coupled[-1]
    for t in range(levels - 1, 0, -1):
        right = ((me >> (t - 1)) & 1) == 1
        mat = jnp.where(right, transfer[t - 1, 1], transfer[t - 1, 0])
        local = coupled[t - 1] + lax.dot_general(
            local,
            mat,
            (((1,), (1,)), ((), ())),
            precision=lax.Precision.HIGHEST,
            preferred_element_type=f32,
        )
    return local.astype(bf16)


def work_list(near_list, me, sign):
    offset = (near_list // LEAVES_DEV - me) * sign
    slot = jnp.zeros_like(offset)
    for n, o in enumerate(SLOT_OFFSETS):
        slot = jnp.where(offset == o, n, slot)
    return slot * LEAVES_DEV + near_list % LEAVES_DEV


def gate_kernel(*refs):
    pass


def gate(array, *after):
    return pl.pallas_call(
        gate_kernel,
        out_shape=jax.ShapeDtypeStruct(array.shape, array.dtype),
        in_specs=[VM] * (1 + len(after)),
        out_specs=VM,
        input_output_aliases={0: 0},
        compiler_params=params(2),
    )(array, *after)


def gate_copy_kernel(array, *refs):
    refs[-1][0] = array[0]


def gate_first(array, *after):
    return pl.pallas_call(
        gate_copy_kernel,
        out_shape=jax.ShapeDtypeStruct((1,) + array.shape[1:], array.dtype),
        in_specs=[VM] * (1 + len(after)),
        out_specs=VM,
        compiler_params=params(2),
    )(array, *after)


def partner(coefs, step):
    return permuted(coefs, lambda i: i ^ (1 << BITS[step]))


def joined_shape(n):
    return jax.ShapeDtypeStruct((n, RHS, RANK), f32)


def local(charges, points, leaf_basis, transfer, coupling, near_list, couple_flags):
    me = lax.axis_index("leaf")
    sign = 1 - 2 * (me % 2)
    place = jnp.stack([me, sign]).astype(jnp.int32)
    work = work_list(near_list, me, sign)

    own = pack(charges, points)
    sib = permuted(own, lambda i: i ^ 1)
    pair = jnp.stack([own, sib])
    coefs = jnp.dot(
        charges,
        leaf_basis.reshape(LEAVES_DEV * LEAF, RANK),
        preferred_element_type=f32,
    )[None]
    recv = partner(coefs, 0)
    following = partner(jnp.concatenate([coefs, recv]), 1)
    acc, tgt, vals, feats, coefs = staged(
        first_kernel,
        [place],
        [own, coefs, recv],
        [],
        [ACC, TGT, VALS, TGT, joined_shape(2)],
        2,
        (TMP,),
    )
    for step in (1, 2):
        recv = following
        following = partner(jnp.concatenate([coefs, recv]), step + 1)
        if step == 2:
            pair = gate(pair, recv)
            near1 = permuted(pair, lambda i: i - 1 if i % 2 == 0 else i + 1)
        acc, coefs = staged(
            functools.partial(own_kernel, step),
            [],
            [tgt, vals, feats, coefs, recv],
            [acc],
            [joined_shape(2 ** (step + 1))],
            SELF[step] - SELF[step - 1],
        )
    recv = following
    near1 = gate(near1, acc, recv)
    near2 = permuted(near1, lambda i: i ^ 1)
    far1 = permuted(near1, lambda i: i - 2 if i % 2 == 0 else i + 2)
    following = partner(jnp.concatenate([coefs, recv]), 4)
    acc, coefs = staged(
        near_kernel,
        [place, work],
        [pair, near1, near2, coefs, recv],
        [acc],
        [joined_shape(16)],
        BUDGET,
        window_scratch(6),
    )
    far2 = permuted(gate_first(far1, acc, following), lambda i: i ^ 1)
    (acc,) = staged(
        last_kernel,
        [place, work],
        [pair, near1, near2, far1],
        [acc],
        [],
        20,
        window_scratch(8),
    )
    return staged(
        tree_kernel,
        [place, work, couple_flags[0]],
        [pair, far2, coefs, following, transfer, coupling, leaf_basis],
        [acc],
        [jax.ShapeDtypeStruct((RHS, LEAVES_DEV * LEAF), bf16)],
        3,
        window_scratch(1),
    )[-1]


def solution(mesh):
    return jax.shard_map(
        local,
        mesh=mesh,
        in_specs=(
            P(None, "leaf"),
            P(None, "leaf"),
            P("leaf", None, None),
            P(),
            P(),
            P("leaf", None),
            P("leaf", None, None),
        ),
        out_specs=P(None, "leaf"),
        check_vma=False,
    )
```

```python
import functools
import math

import jax
import jax.numpy as jnp
from jax import lax
from jax.experimental import pallas as pl
from jax.experimental.pallas import tpu as pltpu
from jax.sharding import PartitionSpec as P

bf16 = jnp.bfloat16
f32 = jnp.float32
smoothing_sq = 0.01
LEAF = 1024
HALF = 512
LEAVES_DEV = 8
RHS = 16
RANK = 128
NB = 5
FEATS = 16
PAYLOAD = (19, 16, HALF)
VM = pl.BlockSpec(memory_space=pltpu.VMEM)
SM = pl.BlockSpec(memory_space=pltpu.SMEM)
SLOT_OFFSETS = (0, 1, -1, -2, 2, 3, -3, -4, 4)
SELF = (1, 3, 8)
BITS = (0, 3, 4, 1, 2)
EARLY = 3
BUDGET = 12


def params(mib):
    return pltpu.CompilerParams(vmem_limit_bytes=mib * 2**20)


def permuted(array, source_of):
    count = lax.axis_size("leaf")
    route = [(source_of(i), i) for i in range(count) if 0 <= source_of(i) < count]
    return lax.ppermute(array, "leaf", route)


def pack_kernel(charges_hbm, points_hbm, out, charges, points, rows, sems):
    get_points = pltpu.make_async_copy(points_hbm, points, sems.at[0])
    get_charges = pltpu.make_async_copy(charges_hbm, charges, sems.at[1])
    get_points.start()
    get_charges.start()
    get_points.wait()
    for l in range(LEAVES_DEV):
        for h in range(2):
            start = l * LEAF + h * HALF
            part = points[:, start : start + HALF].astype(f32)
            for c in range(3):
                row = h * 24 + c * 8 + l
                rows[row : row + 1, :] = part[c : c + 1]
    for k in range(3):
        out[16 + k] = rows[k * 16 : (k + 1) * 16, :].astype(bf16)
    get_charges.wait()
    for k in range(16):
        out[k] = charges[:, k * HALF : (k + 1) * HALF]


def pack(charges, points):
    anywhere = pl.BlockSpec(memory_space=pl.ANY)
    return pl.pallas_call(
        pack_kernel,
        out_shape=jax.ShapeDtypeStruct(PAYLOAD, bf16),
        in_specs=[anywhere] * 2,
        out_specs=VM,
        scratch_shapes=[
            pltpu.VMEM(charges.shape, bf16),
            pltpu.VMEM(points.shape, bf16),
            pltpu.VMEM((48, HALF), f32),
            pltpu.SemaphoreType.DMA((2,)),
        ],
        compiler_params=params(60),
        cost_estimate=pl.CostEstimate(flops=10**6, bytes_accessed=10**6, transcendentals=0),
    )(charges, points)


def coordinates(block):
    rows = jnp.concatenate([block[16], block[17], block[18]], axis=0).astype(f32)
    return jnp.concatenate([rows[:24], rows[24:]], axis=1)


def squared_norm_parts(block, first_leaf, extra):
    pts = coordinates(block)
    leaf = lax.broadcasted_iota(jnp.int32, (LEAVES_DEV, LEAF), 0) + first_leaf
    a = leaf.astype(f32) * (1.0 / 64.0)
    x, y, z = pts[0:8], pts[8:16], pts[16:24]
    full_x = x + a
    norm = full_x * full_x + y * y + z * z + extra
    high = norm.astype(bf16).astype(f32)
    rest = norm - high
    middle = rest.astype(bf16).astype(f32)
    return x, a, y, z, high, middle, rest - middle


def store_features(dst, base, rows, tmp):
    for f, row in rows:
        tmp[:, f, :] = row
    for l in range(LEAVES_DEV):
        dst[base + l] = tmp[l].astype(bf16)


def constant_rows(tmp, ones):
    for f in range(FEATS):
        if f in ones:
            tmp[:, f, :] = jnp.ones((LEAVES_DEV, LEAF), f32)
        elif f >= 12:
            tmp[:, f, :] = jnp.zeros((LEAVES_DEV, LEAF), f32)


def source_features(block, first_leaf, dst, base, tmp):
    x, a, y, z, high, middle, low = squared_norm_parts(block, first_leaf, 0.0)
    store_features(dst, base, list(enumerate([x, x, a, a, y, z, high, middle, low])), tmp)


def target_features(block, dst, tmp):
    x, a, y, z, high, middle, low = squared_norm_parts(block, 0, smoothing_sq)
    rows = list(enumerate([-2 * x, -2 * a, -2 * x, -2 * a, -2 * y, -2 * z]))
    store_features(dst, 0, rows + [(9, high), (10, middle), (11, low)], tmp)


def load_cluster(block, slot, sign, vals, feats, tmp, window_slot=None):
    for l in range(LEAVES_DEV):
        vals[slot * LEAVES_DEV + l, :, :HALF] = block[2 * l]
        vals[slot * LEAVES_DEV + l, :, HALF:] = block[2 * l + 1]
    offset = SLOT_OFFSETS[slot if window_slot is None else window_slot]
    first_leaf = offset * LEAVES_DEV * sign
    source_features(block, first_leaf, feats, slot * LEAVES_DEV, tmp)


def add_block(i, w, tgt, vals, feats, acc):
    src = feats[w].astype(f32).T.astype(bf16)
    dist_sq = jnp.dot(src, tgt[i], preferred_element_type=f32)
    kernel_vals = lax.rsqrt(dist_sq).astype(bf16)
    acc[i] += jnp.dot(vals[w], kernel_vals, preferred_element_type=f32)


def add_listed(part, work, items, tgt, vals, feats, acc):
    def select(it, counts):
        early, first, chosen = counts
        i, k = it // (NB - 1), it % (NB - 1) + 1
        w = work[i, k]
        in_early = (w < 2 * LEAVES_DEV) & (early < EARLY)
        in_first = jnp.logical_not(in_early) & (w < 6 * LEAVES_DEV) & (first < BUDGET)
        in_last = w >= 8 * LEAVES_DEV
        in_part = (
            in_early,
            in_first,
            jnp.logical_not(in_early | in_first | in_last),
            in_last,
        )[part]
        items[chosen] = i * 128 + w
        return (
            early + in_early.astype(jnp.int32),
            first + in_first.astype(jnp.int32),
            chosen + in_part.astype(jnp.int32),
        )

    _, _, count = lax.fori_loop(0, LEAVES_DEV * (NB - 1), select, (jnp.int32(0),) * 3)
    base = 8 * LEAVES_DEV if part == 3 else 0

    def several(group):
        def some(g, carry):
            for u in range(group):
                item = items[g * group + u]
                add_block(item // 128, item % 128 - base, tgt, vals, feats, acc)
            return carry

        return some

    whole = count // 4
    lax.fori_loop(0, whole, several(4), 0)
    lax.fori_loop(whole * 4, count, several(1), 0)


def own_blocks(first, last, tgt, vals, feats, acc):
    def pair_of_blocks(n, carry):
        for u in range(2):
            i = first + n * 2 + u
            add_block(i, i, tgt, vals, feats, acc)
        return carry

    lax.fori_loop(0, (last - first) // 2, pair_of_blocks, 0)
    if (last - first) % 2 == 1:
        add_block(last - 1, last - 1, tgt, vals, feats, acc)


def join(mine, theirs, joined):
    n = mine.shape[0]
    joined[:n] = mine[...]
    joined[n:] = theirs[...]


def first_kernel(place, own, mine, theirs, acc, tgt, vals, feats, joined, tmp):
    join(mine, theirs, joined)
    acc[...] = jnp.zeros_like(acc)
    constant_rows(tmp, (6, 7, 8))
    target_features(own, tgt, tmp)
    constant_rows(tmp, (9, 10, 11))
    load_cluster(own, 0, place[1], vals, feats, tmp)
    own_blocks(0, SELF[0], tgt, vals, feats, acc)


def own_kernel(step, tgt, vals, feats, mine, theirs, acc_in, acc, joined):
    join(mine, theirs, joined)
    own_blocks(SELF[step - 1], SELF[step], tgt, vals, feats, acc)


def early_kernel(
    place, work, pair, mine, theirs, acc_in, acc, joined, vals, feats, tmp, tgt, items
):
    join(mine, theirs, joined)
    constant_rows(tmp, (6, 7, 8))
    target_features(pair.at[0], tgt, tmp)
    load_clusters([pair], place[1], vals, feats, tmp)
    own_blocks(SELF[1], SELF[2], tgt, vals, feats, acc)
    add_listed(0, work, items, tgt, vals, feats, acc)


def load_clusters(pieces, sign, vals, feats, tmp):
    constant_rows(tmp, (9, 10, 11))
    slot = 0
    for piece in pieces:
        for part in range(piece.shape[0]):
            load_cluster(piece.at[part], slot, sign, vals, feats, tmp)
            slot += 1


def near_kernel(
    place, work, pair, near1, near2, mine, theirs, acc_in, acc, joined, vals, feats, tmp, tgt, items
):
    join(mine, theirs, joined)
    constant_rows(tmp, (6, 7, 8))
    target_features(pair.at[0], tgt, tmp)
    load_clusters([pair, near1, near2], place[1], vals, feats, tmp)
    add_listed(1, work, items, tgt, vals, feats, acc)


def last_kernel(place, work, pair, near1, near2, far1, acc_in, acc, vals, feats, tmp, tgt, items):
    constant_rows(tmp, (6, 7, 8))
    target_features(pair.at[0], tgt, tmp)
    load_clusters([pair, near1, near2, far1], place[1], vals, feats, tmp)
    add_listed(2, work, items, tgt, vals, feats, acc)


def tree_kernel(
    place, work, flags, pair, far2, mine, theirs, transfer, coupling, basis, acc_in,
    acc, out, vals, feats, tmp, tgt, items,
):
    constant_rows(tmp, (6, 7, 8))
    target_features(pair.at[0], tgt, tmp)
    constant_rows(tmp, (9, 10, 11))
    load_cluster(far2.at[0], 0, place[1], vals, feats, tmp, 8)
    add_listed(3, work, items, tgt, vals, feats, acc)
    n = mine.shape[0]
    coefs = []
    for m in range(2 * n):
        where = sum(((m >> bit) & 1) << at for at, bit in enumerate(BITS))
        coefs.append(mine[where] if where < n else theirs[where - n])
    down = tree(place[0], flags, coefs, transfer, coupling)
    scale = 1.0 / math.sqrt(NB * LEAF)
    for l in range(LEAVES_DEV):
        far = lax.dot_general(
            down, basis[l], (((1,), (1,)), ((), ())), preferred_element_type=f32
        )
        out[:, l * LEAF : (l + 1) * LEAF] = (acc[l] * scale + far).astype(bf16)


ACC = jax.ShapeDtypeStruct((LEAVES_DEV, RHS, LEAF), f32)
TMP = pltpu.VMEM((LEAVES_DEV, FEATS, LEAF), f32)


def window_scratch(slots):
    return (
        pltpu.VMEM((slots * LEAVES_DEV, RHS, LEAF), bf16),
        pltpu.VMEM((slots * LEAVES_DEV, FEATS, LEAF), bf16),
        TMP,
        pltpu.VMEM((LEAVES_DEV, FEATS, LEAF), bf16),
        pltpu.SMEM((LEAVES_DEV * NB,), jnp.int32),
    )


TGT = jax.ShapeDtypeStruct((LEAVES_DEV, FEATS, LEAF), bf16)
VALS = jax.ShapeDtypeStruct((LEAVES_DEV, RHS, LEAF), bf16)


def staged(kernel, smem, inputs, state, outs, blocks, scratch=(), unplaced=0):
    ins = len(smem) + len(inputs)
    state_shapes = [jax.ShapeDtypeStruct(s.shape, s.dtype) for s in state]
    return pl.pallas_call(
        kernel,
        out_shape=tuple(state_shapes) + tuple(outs),
        in_specs=[SM] * len(smem)
        + [VM] * (len(inputs) - unplaced)
        + [pl.BlockSpec(memory_space=pl.ANY)] * unplaced
        + [VM] * len(state),
        out_specs=(VM,) * (len(state) + len(outs)),
        scratch_shapes=list(scratch),
        input_output_aliases={ins + n: n for n in range(len(state))},
        compiler_params=params(16),
        cost_estimate=pl.CostEstimate(
            flops=blocks * 10**9, bytes_accessed=10**6, transcendentals=blocks * 10**6
        ),
    )(*smem, *inputs, *state)


def tree(me, flags, coefs, transfer, coupling):
    def dot(a, b):
        return jnp.dot(a, b, precision=lax.Precision.HIGHEST, preferred_element_type=f32)

    levels = 4
    cur = coefs
    coupled = []
    for t in range(levels):
        chosen = [flags[t, m].astype(f32) * cur[m + 1] for m in range(3)]
        coupled.append(
            dot(jnp.concatenate(chosen, axis=1), coupling[t].reshape(3 * RANK, RANK))
        )
        if t + 1 < levels:
            right = ((me >> t) & 1) == 1
            even = jnp.concatenate(cur[0::2], axis=0)
            odd = jnp.concatenate(cur[1::2], axis=0)
            both = jnp.concatenate(
                [jnp.where(right, odd, even), jnp.where(right, even, odd)], axis=1
            )
            merged = dot(both, transfer[t].reshape(2 * RANK, RANK))
            cur = [merged[m * RHS : (m + 1) * RHS] for m in range(len(cur) // 2)]
    local = coupled[-1]
    for t in range(levels - 1, 0, -1):
        right = ((me >> (t - 1)) & 1) == 1
        mat = jnp.where(right, transfer[t - 1, 1], transfer[t - 1, 0])
        local = coupled[t - 1] + lax.dot_general(
            local,
            mat,
            (((1,), (1,)), ((), ())),
            precision=lax.Precision.HIGHEST,
            preferred_element_type=f32,
        )
    return local.astype(bf16)


def work_list(near_list, me, sign):
    offset = (near_list // LEAVES_DEV - me) * sign
    slot = jnp.zeros_like(offset)
    for n, o in enumerate(SLOT_OFFSETS):
        slot = jnp.where(offset == o, n, slot)
    return slot * LEAVES_DEV + near_list % LEAVES_DEV


def gate_kernel(*refs):
    pass


def gate(array, *after):
    return pl.pallas_call(
        gate_kernel,
        out_shape=jax.ShapeDtypeStruct(array.shape, array.dtype),
        in_specs=[VM] * (1 + len(after)),
        out_specs=VM,
        input_output_aliases={0: 0},
        compiler_params=params(2),
    )(array, *after)


def gate_copy_kernel(array, *refs):
    refs[-1][0] = array[0]


def gate_first(array, *after):
    return pl.pallas_call(
        gate_copy_kernel,
        out_shape=jax.ShapeDtypeStruct((1,) + array.shape[1:], array.dtype),
        in_specs=[VM] * (1 + len(after)),
        out_specs=VM,
        compiler_params=params(2),
    )(array, *after)


def partner(coefs, step):
    return permuted(coefs, lambda i: i ^ (1 << BITS[step]))


def joined_shape(n):
    return jax.ShapeDtypeStruct((n, RHS, RANK), f32)


def local(charges, points, leaf_basis, transfer, coupling, near_list, couple_flags):
    me = lax.axis_index("leaf")
    sign = 1 - 2 * (me % 2)
    place = jnp.stack([me, sign]).astype(jnp.int32)
    work = work_list(near_list, me, sign)

    own = pack(charges, points)
    sib = permuted(own, lambda i: i ^ 1)
    pair = jnp.stack([own, sib])
    coefs = jnp.dot(
        charges,
        leaf_basis.reshape(LEAVES_DEV * LEAF, RANK),
        preferred_element_type=f32,
    )[None]
    recv = partner(coefs, 0)
    following = partner(jnp.concatenate([coefs, recv]), 1)
    acc, tgt, vals, feats, coefs = staged(
        first_kernel,
        [place],
        [own, coefs, recv],
        [],
        [ACC, TGT, VALS, TGT, joined_shape(2)],
        2,
        (TMP,),
    )
    for step in (1, 2):
        recv = following
        following = partner(jnp.concatenate([coefs, recv]), step + 1)
        if step == 2:
            pair = gate(pair, recv)
            near1 = permuted(pair, lambda i: i - 1 if i % 2 == 0 else i + 1)
        if step == 1:
            acc, coefs = staged(
                functools.partial(own_kernel, step),
                [],
                [tgt, vals, feats, coefs, recv],
                [acc],
                [joined_shape(4)],
                SELF[1] - SELF[0],
            )
        else:
            acc, coefs = staged(
                early_kernel,
                [place, work],
                [pair, coefs, recv],
                [acc],
                [joined_shape(8)],
                SELF[2] - SELF[1] + EARLY,
                window_scratch(2),
            )
    recv = following
    near1 = gate(near1, acc, recv)
    near2 = permuted(near1, lambda i: i ^ 1)
    far1 = permuted(near1, lambda i: i - 2 if i % 2 == 0 else i + 2)
    following = partner(jnp.concatenate([coefs, recv]), 4)
    acc, coefs = staged(
        near_kernel,
        [place, work],
        [pair, near1, near2, coefs, recv],
        [acc],
        [joined_shape(16)],
        BUDGET,
        window_scratch(6),
    )
    far2 = permuted(gate_first(far1, acc, following), lambda i: i ^ 1)
    (acc,) = staged(
        last_kernel,
        [place, work],
        [pair, near1, near2, far1],
        [acc],
        [],
        20,
        window_scratch(8),
    )
    return staged(
        tree_kernel,
        [place, work, couple_flags[0]],
        [pair, far2, coefs, following, transfer, coupling, leaf_basis],
        [acc],
        [jax.ShapeDtypeStruct((RHS, LEAVES_DEV * LEAF), bf16)],
        3,
        window_scratch(1),
    )[-1]


def solution(mesh):
    return jax.shard_map(
        local,
        mesh=mesh,
        in_specs=(
            P(None, "leaf"),
            P(None, "leaf"),
            P("leaf", None, None),
            P(),
            P(),
            P("leaf", None),
            P("leaf", None, None),
        ),
        out_specs=P(None, "leaf"),
        check_vma=False,
    )
```

```python
import functools
import math

import jax
import jax.numpy as jnp
from jax import lax
from jax.experimental import pallas as pl
from jax.experimental.pallas import tpu as pltpu
from jax.sharding import PartitionSpec as P

bf16 = jnp.bfloat16
f32 = jnp.float32
smoothing_sq = 0.01
LEAF = 1024
HALF = 512
LEAVES_DEV = 8
RHS = 16
RANK = 128
NB = 5
FEATS = 16
PAYLOAD = (19, 16, HALF)
VM = pl.BlockSpec(memory_space=pltpu.VMEM)
SM = pl.BlockSpec(memory_space=pltpu.SMEM)
SLOT_OFFSETS = (0, 1, -1, -2, 2, 3, -3, -4, 4)
SELF = (1, 3, 8)
BITS = (0, 3, 4, 1, 2)
EARLY = 3
BUDGET = 12


def params(mib):
    return pltpu.CompilerParams(vmem_limit_bytes=mib * 2**20)


def permuted(array, source_of):
    count = lax.axis_size("leaf")
    route = [(source_of(i), i) for i in range(count) if 0 <= source_of(i) < count]
    return lax.ppermute(array, "leaf", route)


def pack_kernel(charges, points, out, rows):
    for k in range(16):
        out[k] = charges[:, k * HALF : (k + 1) * HALF]
    for l in range(LEAVES_DEV):
        for h in range(2):
            start = l * LEAF + h * HALF
            part = points[:, start : start + HALF].astype(f32)
            for c in range(3):
                row = h * 24 + c * 8 + l
                rows[row : row + 1, :] = part[c : c + 1]
    for k in range(3):
        out[16 + k] = rows[k * 16 : (k + 1) * 16, :].astype(bf16)


def pack(charges, points):
    return pl.pallas_call(
        pack_kernel,
        out_shape=jax.ShapeDtypeStruct(PAYLOAD, bf16),
        in_specs=[VM, VM],
        out_specs=VM,
        scratch_shapes=[pltpu.VMEM((48, HALF), f32)],
        compiler_params=params(4),
        cost_estimate=pl.CostEstimate(flops=10**6, bytes_accessed=10**6, transcendentals=0),
    )(charges, points)


def coordinates(block):
    rows = jnp.concatenate([block[16], block[17], block[18]], axis=0).astype(f32)
    return jnp.concatenate([rows[:24], rows[24:]], axis=1)


def squared_norm_parts(block, first_leaf, extra):
    pts = coordinates(block)
    leaf = lax.broadcasted_iota(jnp.int32, (LEAVES_DEV, LEAF), 0) + first_leaf
    a = leaf.astype(f32) * (1.0 / 64.0)
    x, y, z = pts[0:8], pts[8:16], pts[16:24]
    full_x = x + a
    norm = full_x * full_x + y * y + z * z + extra
    high = norm.astype(bf16).astype(f32)
    rest = norm - high
    middle = rest.astype(bf16).astype(f32)
    return x, a, y, z, high, middle, rest - middle


def store_features(dst, base, rows, tmp):
    for f, row in rows:
        tmp[:, f, :] = row
    for l in range(LEAVES_DEV):
        dst[base + l] = tmp[l].astype(bf16)


def constant_rows(tmp, ones):
    for f in range(FEATS):
        if f in ones:
            tmp[:, f, :] = jnp.ones((LEAVES_DEV, LEAF), f32)
        elif f >= 12:
            tmp[:, f, :] = jnp.zeros((LEAVES_DEV, LEAF), f32)


def source_features(block, first_leaf, dst, base, tmp):
    x, a, y, z, high, middle, low = squared_norm_parts(block, first_leaf, 0.0)
    store_features(dst, base, list(enumerate([x, x, a, a, y, z, high, middle, low])), tmp)


def target_features(block, dst, tmp):
    x, a, y, z, high, middle, low = squared_norm_parts(block, 0, smoothing_sq)
    rows = list(enumerate([-2 * x, -2 * a, -2 * x, -2 * a, -2 * y, -2 * z]))
    store_features(dst, 0, rows + [(9, high), (10, middle), (11, low)], tmp)


def load_cluster(block, slot, sign, vals, feats, tmp, window_slot=None):
    for l in range(LEAVES_DEV):
        vals[slot * LEAVES_DEV + l, :, :HALF] = block[2 * l]
        vals[slot * LEAVES_DEV + l, :, HALF:] = block[2 * l + 1]
    offset = SLOT_OFFSETS[slot if window_slot is None else window_slot]
    first_leaf = offset * LEAVES_DEV * sign
    source_features(block, first_leaf, feats, slot * LEAVES_DEV, tmp)


def add_block(i, w, tgt, vals, feats, acc):
    src = feats[w].astype(f32).T.astype(bf16)
    dist_sq = jnp.dot(src, tgt[i], preferred_element_type=f32)
    kernel_vals = lax.rsqrt(dist_sq).astype(bf16)
    acc[i] += jnp.dot(vals[w], kernel_vals, preferred_element_type=f32)


def add_listed(part, work, items, tgt, vals, feats, acc):
    def select(it, counts):
        early, first, chosen = counts
        i, k = it // (NB - 1), it % (NB - 1) + 1
        w = work[i, k]
        in_early = (w < 2 * LEAVES_DEV) & (early < EARLY)
        in_first = jnp.logical_not(in_early) & (w < 6 * LEAVES_DEV) & (first < BUDGET)
        in_last = w >= 8 * LEAVES_DEV
        in_part = (
            in_early,
            in_first,
            jnp.logical_not(in_early | in_first | in_last),
            in_last,
        )[part]
        items[chosen] = i * 128 + w
        return (
            early + in_early.astype(jnp.int32),
            first + in_first.astype(jnp.int32),
            chosen + in_part.astype(jnp.int32),
        )

    _, _, count = lax.fori_loop(0, LEAVES_DEV * (NB - 1), select, (jnp.int32(0),) * 3)
    base = 8 * LEAVES_DEV if part == 3 else 0

    def several(group):
        def some(g, carry):
            for u in range(group):
                item = items[g * group + u]
                add_block(item // 128, item % 128 - base, tgt, vals, feats, acc)
            return carry

        return some

    whole = count // 4
    lax.fori_loop(0, whole, several(4), 0)
    lax.fori_loop(whole * 4, count, several(1), 0)


def own_blocks(first, last, tgt, vals, feats, acc):
    def pair_of_blocks(n, carry):
        for u in range(2):
            i = first + n * 2 + u
            add_block(i, i, tgt, vals, feats, acc)
        return carry

    lax.fori_loop(0, (last - first) // 2, pair_of_blocks, 0)
    if (last - first) % 2 == 1:
        add_block(last - 1, last - 1, tgt, vals, feats, acc)


def join(mine, theirs, joined):
    n = mine.shape[0]
    joined[:n] = mine[...]
    joined[n:] = theirs[...]


def first_kernel(place, own, mine, theirs, acc, tgt, vals, feats, joined, tmp):
    join(mine, theirs, joined)
    acc[...] = jnp.zeros_like(acc)
    constant_rows(tmp, (6, 7, 8))
    target_features(own, tgt, tmp)
    constant_rows(tmp, (9, 10, 11))
    load_cluster(own, 0, place[1], vals, feats, tmp)
    own_blocks(0, SELF[0], tgt, vals, feats, acc)


def own_kernel(step, tgt, vals, feats, mine, theirs, acc_in, acc, joined):
    join(mine, theirs, joined)
    own_blocks(SELF[step - 1], SELF[step], tgt, vals, feats, acc)


def early_kernel(
    place, work, pair, mine, theirs, acc_in, acc, joined, vals, feats, tmp, tgt, items
):
    join(mine, theirs, joined)
    constant_rows(tmp, (6, 7, 8))
    target_features(pair.at[0], tgt, tmp)
    load_clusters([pair], place[1], vals, feats, tmp)
    own_blocks(SELF[1], SELF[2], tgt, vals, feats, acc)
    add_listed(0, work, items, tgt, vals, feats, acc)


def load_clusters(pieces, sign, vals, feats, tmp):
    constant_rows(tmp, (9, 10, 11))
    slot = 0
    for piece in pieces:
        for part in range(piece.shape[0]):
            load_cluster(piece.at[part], slot, sign, vals, feats, tmp)
            slot += 1


def near_kernel(
    place, work, pair, near1, near2, mine, theirs, acc_in, acc, joined, vals, feats, tmp, tgt, items
):
    join(mine, theirs, joined)
    constant_rows(tmp, (6, 7, 8))
    target_features(pair.at[0], tgt, tmp)
    load_clusters([pair, near1, near2], place[1], vals, feats, tmp)
    add_listed(1, work, items, tgt, vals, feats, acc)


def last_kernel(place, work, pair, near1, near2, far1, acc_in, acc, vals, feats, tmp, tgt, items):
    constant_rows(tmp, (6, 7, 8))
    target_features(pair.at[0], tgt, tmp)
    load_clusters([pair, near1, near2, far1], place[1], vals, feats, tmp)
    add_listed(2, work, items, tgt, vals, feats, acc)


def tree_kernel(
    place, work, flags, pair, far2, mine, theirs, transfer, coupling, basis, acc_in,
    acc, out, vals, feats, tmp, tgt, items,
):
    constant_rows(tmp, (6, 7, 8))
    target_features(pair.at[0], tgt, tmp)
    constant_rows(tmp, (9, 10, 11))
    load_cluster(far2.at[0], 0, place[1], vals, feats, tmp, 8)
    add_listed(3, work, items, tgt, vals, feats, acc)
    n = mine.shape[0]
    coefs = []
    for m in range(2 * n):
        where = sum(((m >> bit) & 1) << at for at, bit in enumerate(BITS))
        coefs.append(mine[where] if where < n else theirs[where - n])
    down = tree(place[0], flags, coefs, transfer, coupling)
    scale = 1.0 / math.sqrt(NB * LEAF)
    for l in range(LEAVES_DEV):
        far = lax.dot_general(
            down, basis[l], (((1,), (1,)), ((), ())), preferred_element_type=f32
        )
        out[:, l * LEAF : (l + 1) * LEAF] = (acc[l] * scale + far).astype(bf16)


ACC = jax.ShapeDtypeStruct((LEAVES_DEV, RHS, LEAF), f32)
TMP = pltpu.VMEM((LEAVES_DEV, FEATS, LEAF), f32)


def window_scratch(slots):
    return (
        pltpu.VMEM((slots * LEAVES_DEV, RHS, LEAF), bf16),
        pltpu.VMEM((slots * LEAVES_DEV, FEATS, LEAF), bf16),
        TMP,
        pltpu.VMEM((LEAVES_DEV, FEATS, LEAF), bf16),
        pltpu.SMEM((LEAVES_DEV * NB,), jnp.int32),
    )


TGT = jax.ShapeDtypeStruct((LEAVES_DEV, FEATS, LEAF), bf16)
VALS = jax.ShapeDtypeStruct((LEAVES_DEV, RHS, LEAF), bf16)


def staged(kernel, smem, inputs, state, outs, blocks, scratch=(), unplaced=0):
    ins = len(smem) + len(inputs)
    state_shapes = [jax.ShapeDtypeStruct(s.shape, s.dtype) for s in state]
    return pl.pallas_call(
        kernel,
        out_shape=tuple(state_shapes) + tuple(outs),
        in_specs=[SM] * len(smem)
        + [VM] * (len(inputs) - unplaced)
        + [pl.BlockSpec(memory_space=pl.ANY)] * unplaced
        + [VM] * len(state),
        out_specs=(VM,) * (len(state) + len(outs)),
        scratch_shapes=list(scratch),
        input_output_aliases={ins + n: n for n in range(len(state))},
        compiler_params=params(16),
        cost_estimate=pl.CostEstimate(
            flops=blocks * 10**9, bytes_accessed=10**6, transcendentals=blocks * 10**6
        ),
    )(*smem, *inputs, *state)


def tree(me, flags, coefs, transfer, coupling):
    def dot(a, b):
        return jnp.dot(a, b, precision=lax.Precision.HIGHEST, preferred_element_type=f32)

    levels = 4
    cur = coefs
    coupled = []
    for t in range(levels):
        chosen = [flags[t, m].astype(f32) * cur[m + 1] for m in range(3)]
        coupled.append(
            dot(jnp.concatenate(chosen, axis=1), coupling[t].reshape(3 * RANK, RANK))
        )
        if t + 1 < levels:
            right = ((me >> t) & 1) == 1
            even = jnp.concatenate(cur[0::2], axis=0)
            odd = jnp.concatenate(cur[1::2], axis=0)
            both = jnp.concatenate(
                [jnp.where(right, odd, even), jnp.where(right, even, odd)], axis=1
            )
            merged = dot(both, transfer[t].reshape(2 * RANK, RANK))
            cur = [merged[m * RHS : (m + 1) * RHS] for m in range(len(cur) // 2)]
    local = coupled[-1]
    for t in range(levels - 1, 0, -1):
        right = ((me >> (t - 1)) & 1) == 1
        mat = jnp.where(right, transfer[t - 1, 1], transfer[t - 1, 0])
        local = coupled[t - 1] + lax.dot_general(
            local,
            mat,
            (((1,), (1,)), ((), ())),
            precision=lax.Precision.HIGHEST,
            preferred_element_type=f32,
        )
    return local.astype(bf16)


def work_list(near_list, me, sign):
    offset = (near_list // LEAVES_DEV - me) * sign
    slot = jnp.zeros_like(offset)
    for n, o in enumerate(SLOT_OFFSETS):
        slot = jnp.where(offset == o, n, slot)
    return slot * LEAVES_DEV + near_list % LEAVES_DEV


def gate_kernel(*refs):
    pass


def gate(array, *after):
    return pl.pallas_call(
        gate_kernel,
        out_shape=jax.ShapeDtypeStruct(array.shape, array.dtype),
        in_specs=[VM] * (1 + len(after)),
        out_specs=VM,
        input_output_aliases={0: 0},
        compiler_params=params(2),
    )(array, *after)


def gate_copy_kernel(array, *refs):
    refs[-1][0] = array[0]


def gate_first(array, *after):
    return pl.pallas_call(
        gate_copy_kernel,
        out_shape=jax.ShapeDtypeStruct((1,) + array.shape[1:], array.dtype),
        in_specs=[VM] * (1 + len(after)),
        out_specs=VM,
        compiler_params=params(2),
    )(array, *after)


def partner(coefs, step):
    return permuted(coefs, lambda i: i ^ (1 << BITS[step]))


def joined_shape(n):
    return jax.ShapeDtypeStruct((n, RHS, RANK), f32)


def local(charges, points, leaf_basis, transfer, coupling, near_list, couple_flags):
    me = lax.axis_index("leaf")
    sign = 1 - 2 * (me % 2)
    place = jnp.stack([me, sign]).astype(jnp.int32)
    work = work_list(near_list, me, sign)

    own = pack(charges, points)
    sib = permuted(own, lambda i: i ^ 1)
    pair = jnp.stack([own, sib])
    coefs = jnp.dot(
        charges,
        leaf_basis.reshape(LEAVES_DEV * LEAF, RANK),
        preferred_element_type=f32,
    )[None]
    recv = partner(coefs, 0)
    following = partner(jnp.concatenate([coefs, recv]), 1)
    acc, tgt, vals, feats, coefs = staged(
        first_kernel,
        [place],
        [own, coefs, recv],
        [],
        [ACC, TGT, VALS, TGT, joined_shape(2)],
        2,
        (TMP,),
    )
    for step in (1, 2):
        recv = following
        following = partner(jnp.concatenate([coefs, recv]), step + 1)
        if step == 2:
            pair = gate(pair, recv)
            near1 = permuted(pair, lambda i: i - 1 if i % 2 == 0 else i + 1)
        if step == 1:
            acc, coefs = staged(
                functools.partial(own_kernel, step),
                [],
                [tgt, vals, feats, coefs, recv],
                [acc],
                [joined_shape(4)],
                SELF[1] - SELF[0],
            )
        else:
            acc, coefs = staged(
                early_kernel,
                [place, work],
                [pair, coefs, recv],
                [acc],
                [joined_shape(8)],
                SELF[2] - SELF[1] + EARLY,
                window_scratch(2),
            )
    recv = following
    near1 = gate(near1, acc, recv)
    near2 = permuted(near1, lambda i: i ^ 1)
    far1 = permuted(near1, lambda i: i - 2 if i % 2 == 0 else i + 2)
    following = partner(jnp.concatenate([coefs, recv]), 4)
    acc, coefs = staged(
        near_kernel,
        [place, work],
        [pair, near1, near2, coefs, recv],
        [acc],
        [joined_shape(16)],
        BUDGET,
        window_scratch(6),
    )
    far2 = permuted(gate_first(far1, acc, following), lambda i: i ^ 1)
    (acc,) = staged(
        last_kernel,
        [place, work],
        [pair, near1, near2, far1],
        [acc],
        [],
        20,
        window_scratch(8),
    )
    return staged(
        tree_kernel,
        [place, work, couple_flags[0]],
        [pair, far2, coefs, following, transfer, coupling, leaf_basis],
        [acc],
        [jax.ShapeDtypeStruct((RHS, LEAVES_DEV * LEAF), bf16)],
        3,
        window_scratch(1),
    )[-1]


def solution(mesh):
    return jax.shard_map(
        local,
        mesh=mesh,
        in_specs=(
            P(None, "leaf"),
            P(None, "leaf"),
            P("leaf", None, None),
            P(),
            P(),
            P("leaf", None),
            P("leaf", None, None),
        ),
        out_specs=P(None, "leaf"),
        check_vma=False,
    )
```
